128 devices in a mesh: row: 16 (over y, x_lo, core), col: 8 (over z, x_hi).
Axes of the slice: x: 4 (x_hi: 2, x_lo: 2; x = x_hi * 2 + x_lo), y: 4, z: 4, core: 2. Of those that a mesh axis runs over, the one named last changes fastest.
Arguments:
- eigenvectors: float32 [512, 65536], P(('row', 'col')), may hold values from -6 to 6
- reflectors: float32 [8, 256, 65536], P(None, 'col', 'row'), as said below
Outputs:
- backtransformed: float32 [512, 65536], P('col', 'row')
The draws below stay inside these ranges and needn't reach their ends.
Inputs may be any that keep to these rules, and one draw needn't show every extreme that they name: Row j of reflectors[b] is zero at positions before b * 8192 + j and equals one at that position.
All inputs are finite; a program needn't handle non-finite values.
Results may differ from the reference program's by a relative error of at most 0.0003.
Values sent between devices are 32-bit elements; how exact they have to be, the bound alone decides.
No kernel may reach another device: no remote copies, remote signals or barrier semaphores. Data moves between devices by JAX's collectives and lax.ppermute only.
A program may use at most 128 MiB of HBM per device.

```python
import math
import jax
import jax.numpy as jnp
from jax import lax

N = 65536
NB = 256
NBLK = 8
M = 512
STRIDE = 8192


def draw_reflectors(key, part):
    subkey = jax.random.fold_in(key, 7)
    private_key, common_key = jax.random.split(subkey)
    private_part = jax.random.normal(private_key, (NBLK, NB, N), jnp.float32)
    common_part = jax.random.normal(common_key, (NBLK, 1, N), jnp.float32)
    position = lax.broadcasted_iota(jnp.int32, (NBLK, NB, N), 2)
    first_row = lax.broadcasted_iota(jnp.int32, (NBLK, NB, N), 0) * STRIDE + lax.broadcasted_iota(jnp.int32, (NBLK, NB, N), 1)
    spread_part = (private_part + common_part) * (1.0 / math.sqrt(N))
    values = jnp.where(position > first_row, spread_part, jnp.where(position == first_row, 1.0, 0.0))
    return values.astype(jnp.float32)


def steps_of(stream_key, dims, shards, low, high):
    level, own = 1.0, jax.random.fold_in(stream_key, 6)
    for axis_at, parts in shards:
        steps = jnp.exp(jax.random.uniform(jax.random.fold_in(own, axis_at), (parts,), jnp.float32, low / len(shards), high / len(shards)))
        level = level * jnp.repeat(steps, dims[axis_at] // parts).reshape([-1 if axis == axis_at else 1 for axis in range(len(dims))])
    return level


def noise(rng, dims, scale, limit, cuts=(), held_as=jnp.bfloat16):
    array = scale * jax.random.normal(rng, dims, jnp.float32)
    if cuts:
        array = array * steps_of(rng, dims, cuts, -0.22, 0.18)
    return jnp.clip(array, -limit, limit).astype(held_as)


def setup_inputs(seed: int = 0) -> dict:
    arg_keys = jax.random.split(jax.random.key(seed), 3)
    eigenvectors = noise(arg_keys[0], (M, N), 1.0, 6.0, ((0, 128),), jnp.float32)
    reflectors = draw_reflectors(jax.random.fold_in(arg_keys[2], 71), 0)
    return dict(eigenvectors=eigenvectors, reflectors=reflectors)


HIGHEST = lax.Precision.HIGHEST


def upper_inverse(factor):
    width = factor.shape[-1]
    identity = jnp.eye(width, dtype=jnp.float32)
    diagonal = jnp.sum(factor * identity, axis=-1)
    strict = factor - factor * identity

    def back_step(count, inverse):
        index = (width - 1 - count).astype(jnp.int32)
        row_part = lax.dynamic_slice_in_dim(strict, index, 1, 1)
        unit_row = lax.dynamic_slice_in_dim(identity, index, 1, 0)
        pivot = lax.dynamic_slice_in_dim(diagonal, index, 1, 1)
        solved = jnp.einsum("bij,bjk->bik", row_part, inverse, precision=HIGHEST)
        value = (unit_row[None, :, :] - solved) / pivot[:, :, None]
        return lax.dynamic_update_slice_in_dim(inverse, value, index, 1)

    return lax.fori_loop(jnp.int32(0), jnp.int32(width), back_step, jnp.zeros_like(factor))


def reference(eigenvectors, reflectors):
    gram_total = jnp.einsum("bjn,bkn->bjk", reflectors, reflectors, precision=HIGHEST, preferred_element_type=jnp.float32)
    width = reflectors.shape[1]
    factor = jnp.triu(gram_total, 1) + 0.5 * gram_total * jnp.eye(width, dtype=jnp.float32)
    inverse = upper_inverse(factor)
    current = eigenvectors
    for block_index in range(NBLK - 1, -1, -1):
        vectors = reflectors[block_index]
        projection = jnp.dot(current, vectors.T, precision=HIGHEST, preferred_element_type=jnp.float32)
        coefficients = jnp.dot(projection, inverse[block_index].T, precision=HIGHEST, preferred_element_type=jnp.float32)
        current = current - jnp.dot(coefficients, vectors, precision=HIGHEST, preferred_element_type=jnp.float32)
    return current
```

```python
import jax
import jax.numpy as jnp
from jax import lax
from jax.experimental import pallas as pl
from jax.experimental.pallas import tpu as pltpu
from jax.sharding import Mesh, PartitionSpec as P

AXES = ("y", "xl", "core", "z", "xh")
SIZES = (4, 2, 2, 4, 2)
CHIPS = ("y", "xl", "z", "xh")
COLS = ("z", "xh")
CORE_COLS = ("core", "z", "xh")
SWAP = ((0, 1), (1, 0))

NCHIP = 64
NCOL = 8
NB = 256
GROUP = 4
PAIRS = [(i, j) for i in range(GROUP) for j in range(i, GROUP)]
GROWS = len(PAIRS) * 2 * NB // NCHIP
PROWS = 32
VMEM = pl.BlockSpec(memory_space=pltpu.VMEM)
SMEM = pl.BlockSpec(memory_space=pltpu.SMEM)
F32 = jnp.float32
BF16 = jnp.bfloat16
NT = (((1,), (1,)), ((), ()))
NN = (((1,), (0,)), ((), ()))


def call(kernel, out_shape, scratch=(), limit=50, flops=0, size=0):
    return pl.pallas_call(
        kernel,
        out_shape=out_shape,
        scratch_shapes=list(scratch),
        compiler_params=pltpu.CompilerParams(vmem_limit_bytes=limit * 1024 * 1024),
        cost_estimate=pl.CostEstimate(flops=flops, bytes_accessed=size, transcendentals=0),
    )


def f32(*shape):
    return jax.ShapeDtypeStruct(shape, F32)


def split(value):
    high = value.astype(BF16)
    return high, (value - high.astype(F32)).astype(BF16)


def dot3(a, b, dims):
    def one(x, y):
        return lax.dot_general(x, y, dims, preferred_element_type=F32)

    return one(a[0], b[0]) + (one(a[0], b[1]) + one(a[1], b[0]))


def cut_eigenvectors(e_ref, out_ref):
    for core in range(2):
        for c in range(NCOL):
            for t in range(4):
                for k in range(8):
                    at = (((k * 2 + core) * NCOL + c) * 4 + t) * 128
                    out_ref[k * NCOL + c, core, t * 4 : t * 4 + 4, :] = e_ref[:, at : at + 128]


def cut_vectors(w_ref, out_ref):
    out_ref[0] = w_ref[...]


def split_vectors(own_ref, sib_ref, high_ref, low_ref):
    for part, ref in enumerate((own_ref, sib_ref)):
        for b in range(8):
            for c in range(NCOL):
                high, low = split(ref[c, b])
                high_ref[b, c * 32 : c * 32 + 32, part * 512 : part * 512 + 512] = high
                low_ref[b, c * 32 : c * 32 + 32, part * 512 : part * 512 + 512] = low


def products(core_ref, own_ref, sib_ref, e_ref, buf_ref, high_ref, low_ref, x_ref, eh_ref, el_ref):
    core = core_ref[0]
    split_vectors(own_ref, sib_ref, high_ref, low_ref)
    for part in range(2):
        held = core if part == 0 else 1 - core
        for t in range(4):
            for i in range(4):
                value = e_ref[pl.ds(held * 16 + t * 4 + i, NCHIP, stride=32), :]
                at = part * 512 + t * 128
                x_ref[i * 64 : i * 64 + 64, at : at + 128] = value
                high, low = split(value)
                eh_ref[i * 64 : i * 64 + 64, at : at + 128] = high
                el_ref[i * 64 : i * 64 + 64, at : at + 128] = low
    base = (1 - core) * GROUP
    step = GROWS + PROWS
    for index, (i, j) in enumerate(PAIRS):
        a = (high_ref[base + i], low_ref[base + i])
        b = (high_ref[base + j], low_ref[base + j])
        value = dot3(a, b, NT)
        for half in range(2):
            at = (index * 2 + half) * NB
            done = 0
            while done < NB:
                chip, offset = divmod(at + done, GROWS)
                take = min(NB - done, GROWS - offset)
                start = chip * step + offset
                buf_ref[start : start + take, :] = value[done : done + take, half * 128 : half * 128 + 128]
                done += take
    project((eh_ref[...], el_ref[...]), high_ref, low_ref, GROUP, buf_ref, GROWS, step)


def project(x, high_ref, low_ref, base, buf_ref, offset, step):
    for b in range(GROUP):
        value = dot3(x, (high_ref[base + b], low_ref[base + b]), NT)
        for half in range(2):
            for i in range(4):
                start = offset + (b * 2 + half) * 4 + i
                buf_ref[pl.ds(start, NCHIP, stride=step), :] = value[
                    i * 64 : i * 64 + 64, half * 128 : half * 128 + 128
                ]


def sum_both(buf_ref, g_ref, p_ref):
    def add(q, total):
        return total + buf_ref[q]

    total = lax.fori_loop(0, NCHIP, add, jnp.zeros((GROWS + PROWS, 128), F32), unroll=8)
    p_ref[...] = total[GROWS:]
    part = total[:GROWS]

    def spread(q, carry):
        g_ref[q] = part
        return carry

    lax.fori_loop(0, NCHIP, spread, 0, unroll=8)


def sum_projection(buf_ref, p_ref):
    def add(q, total):
        return total + buf_ref[q]

    p_ref[...] = lax.fori_loop(0, NCHIP, add, jnp.zeros((PROWS, 128), F32), unroll=8)


def block_of(g_ref, index):
    at = index * 2 * NB
    return jnp.concatenate([g_ref[at : at + NB, :], g_ref[at + NB : at + 2 * NB, :]], axis=1)


def exact(a, b, dims):
    return lax.dot_general(a, b, dims, precision=lax.Precision.HIGHEST, preferred_element_type=F32)


def upper_inverse(gram):
    row = lax.broadcasted_iota(jnp.int32, (NB, NB), 0)
    col = lax.broadcasted_iota(jnp.int32, (NB, NB), 1)
    same = row == col
    diagonal = jnp.where(same, 0.5 * gram, 0.0)
    strict = jnp.where(row < col, gram, 0.0)
    down = 1.0 / jnp.sum(diagonal, axis=1, keepdims=True)
    across = 1.0 / jnp.sum(diagonal, axis=0, keepdims=True)
    apart = row ^ col
    inverse = jnp.where(same, down, 0.0) - down * jnp.where(apart == 1, strict, 0.0) * across
    size = 2
    while size < NB:
        beside = jnp.where((apart >= size) & (apart < 2 * size), strict, 0.0)
        inverse = inverse - exact(exact(inverse, beside, NN), inverse, NN)
        size *= 2
    return inverse


def solve(g_ref, inv_ref, own_ref, sib_ref, c_own_ref, c_sib_ref):
    def rows(b):
        parts = []
        for half in range(2):
            t = b * 2 + half
            parts.append(jnp.concatenate([own_ref[t * 4 : t * 4 + 4, :], sib_ref[t * 4 : t * 4 + 4, :]], axis=0))
        return jnp.concatenate(parts, axis=1)

    found = {}
    for b in range(GROUP - 1, -1, -1):
        rest = rows(b)
        for later in range(GROUP - 1, b, -1):
            rest = rest - exact(found[later], block_of(g_ref, PAIRS.index((b, later))), NT)
        found[b] = exact(rest, inv_ref[b], NT)
        for half in range(2):
            t = b * 2 + half
            c_own_ref[t * 4 : t * 4 + 4, :] = found[b][0:4, half * 128 : half * 128 + 128]
            c_sib_ref[t * 4 : t * 4 + 4, :] = found[b][4:8, half * 128 : half * 128 + 128]


def invert_and_solve(g_ref, own_ref, sib_ref, inv_ref, c_own_ref, c_sib_ref):
    for b in range(GROUP):
        inv_ref[b] = upper_inverse(block_of(g_ref, PAIRS.index((b, b))))
    solve(g_ref, inv_ref, own_ref, sib_ref, c_own_ref, c_sib_ref)


def updated(c_ref, high_ref, low_ref, x_ref, ch_ref, cl_ref, base, part):
    if part == 0:
        for t in range(8):
            for i in range(4):
                high, low = split(c_ref[pl.ds(t * 4 + i, NCHIP, stride=PROWS), :])
                ch_ref[i * 64 : i * 64 + 64, t * 128 : t * 128 + 128] = high
                cl_ref[i * 64 : i * 64 + 64, t * 128 : t * 128 + 128] = low
    at = part * 512
    value = x_ref[:, at : at + 512]
    for b in range(GROUP):
        c = (ch_ref[:, b * NB : b * NB + NB], cl_ref[:, b * NB : b * NB + NB])
        w = (high_ref[base + b, :, at : at + 512], low_ref[base + b, :, at : at + 512])
        value = value - dot3(c, w, NN)
    return value


def update_and_project(c_ref, high_ref, low_ref, x_ref, out_ref, buf_ref, ch_ref, cl_ref, xh_ref, xl_ref):
    for part in range(2):
        value = updated(c_ref, high_ref, low_ref, x_ref, ch_ref, cl_ref, GROUP, part)
        out_ref[:, part * 512 : part * 512 + 512] = value
        high, low = split(value)
        xh_ref[:, part * 512 : part * 512 + 512] = high
        xl_ref[:, part * 512 : part * 512 + 512] = low
    project((xh_ref[...], xl_ref[...]), high_ref, low_ref, 0, buf_ref, 0, PROWS)


def update_last(core_ref, c_ref, high_ref, low_ref, x_ref, out_ref, ch_ref, cl_ref):
    core = core_ref[0]
    for part in range(2):
        value = updated(c_ref, high_ref, low_ref, x_ref, ch_ref, cl_ref, 0, part)
        held = core if part == 0 else 1 - core
        for c in range(NCOL):
            for i in range(4):
                out_ref[held * NCOL + c, i * 8 : i * 8 + 8, :] = value[i * 64 + c * 8 : i * 64 + c * 8 + 8, :]


def place_rows(in_ref, out_ref, held_ref):
    for c in range(NCOL):
        for t in range(4):
            at = c * 512 + t * 128
            for core in range(2):
                for i in range(4):
                    held_ref[pl.ds((c * 4 + t) * 64 + core * 32 + i, 8, stride=4), :] = in_ref[
                        core * NCOL + c, i * 8 : i * 8 + 8, t * 128 : t * 128 + 128
                    ]
            out_ref[:, at : at + 128] = held_ref[(c * 4 + t) * 64 : (c * 4 + t) * 64 + 64, :]


def with_core(kernel, out_shape, scratch, count, **costs):
    return pl.pallas_call(
        kernel,
        out_shape=out_shape,
        in_specs=[SMEM] + [VMEM] * count,
        scratch_shapes=list(scratch),
        compiler_params=pltpu.CompilerParams(vmem_limit_bytes=50 * 1024 * 1024),
        cost_estimate=pl.CostEstimate(transcendentals=0, **costs),
    )


def exchange(value, axes):
    return lax.all_to_all(value, axes, 0, 0, tiled=True)


def on_device(eigenvectors, reflectors):
    core = lax.axis_index("core").astype(jnp.int32)
    which = core.reshape(1)
    half = [pltpu.VMEM((256, 1024), BF16)] * 2

    vectors = pl.pallas_call(
        cut_vectors,
        grid=(NCOL,),
        in_specs=[pl.BlockSpec((8, 32, 512), lambda c: (0, 0, c))],
        out_specs=pl.BlockSpec((1, 8, 32, 512), lambda c: (c, 0, 0, 0)),
        out_shape=f32(NCOL, 8, 32, 512),
        compiler_params=pltpu.CompilerParams(vmem_limit_bytes=16 * 1024 * 1024),
    )(reflectors)
    own = exchange(vectors, COLS)
    sib = lax.ppermute(own, "core", SWAP)
    pieces = call(cut_eigenvectors, f32(NCHIP, 2, 16, 128))(eigenvectors)
    spread = exchange(pieces, CHIPS).reshape(NCHIP * 32, 128)

    split_shape = jax.ShapeDtypeStruct((8, NB, 1024), BF16)
    step = GROWS + PROWS
    buf, high, low, start = with_core(
        products,
        (f32(NCHIP * step, 128), split_shape, split_shape, f32(256, 1024)),
        half,
        3,
        flops=6 * 10**9,
        bytes_accessed=22 * 2**20,
    )(which, own, sib, spread)
    arrived = exchange(buf.reshape(NCHIP, step, 128), CHIPS)
    gram, projection = call(sum_both, (f32(NCHIP, GROWS, 128), f32(PROWS, 128)))(arrived)
    gram = exchange(gram, CHIPS).reshape(NCHIP * GROWS, 128)

    def spread_rows(mine, other, owner):
        passed = lax.ppermute(other, "core", SWAP)
        rows = jnp.where(core == owner, mine, passed)
        rows = jnp.broadcast_to(rows[None], (NCHIP, PROWS, 128))
        return exchange(rows, CHIPS).reshape(NCHIP * PROWS, 128)

    rows = f32(PROWS, 128)
    inverse, mine, other = call(invert_and_solve, (f32(GROUP, NB, NB), rows, rows))(
        gram, projection, lax.ppermute(projection, "core", SWAP)
    )
    coefficients = spread_rows(mine, other, 0)
    middle, buf = call(update_and_project, (f32(256, 1024), f32(NCHIP * PROWS, 128)), half * 2)(
        coefficients, high, low, start
    )
    arrived = exchange(buf.reshape(NCHIP, PROWS, 128), CHIPS)
    projection = call(sum_projection, rows)(arrived)
    mine, other = call(solve, (rows, rows))(
        gram, inverse, projection, lax.ppermute(projection, "core", SWAP)
    )
    coefficients = spread_rows(mine, other, 1)
    finished = with_core(
        update_last, f32(2 * NCOL, 32, 512), half, 4, flops=2 * 10**9, bytes_accessed=8 * 2**20
    )(which, coefficients, high, low, middle)
    return call(place_rows, f32(64, 4096), [pltpu.VMEM((2048, 128), F32)])(exchange(finished, CORE_COLS))


def solution(mesh):
    fine = Mesh(mesh.devices.reshape(SIZES), AXES)
    in_specs = (P(AXES, None), P(None, COLS, ("y", "xl", "core")))
    out_specs = P(COLS, ("y", "xl", "core"))
    return jax.shard_map(on_device, mesh=fine, in_specs=in_specs, out_specs=out_specs, check_vma=False)
```

```python
import jax
import jax.numpy as jnp
from jax import lax
from jax.experimental import pallas as pl
from jax.experimental.pallas import tpu as pltpu
from jax.sharding import Mesh, PartitionSpec as P

AXES = ("y", "xl", "core", "z", "xh")
SIZES = (4, 2, 2, 4, 2)
CHIPS = ("y", "xl", "z", "xh")
COLS = ("z", "xh")
CORE_COLS = ("core", "z", "xh")
SWAP = ((0, 1), (1, 0))

NCHIP = 64
NCOL = 8
NB = 256
GROUP = 4
PAIRS = [(i, j) for i in range(GROUP) for j in range(i, GROUP)]


def place_pieces():
    at, pieces = 0, {}
    for i, j in PAIRS:
        for half in range(2):
            rows = NB // 2 if i == j and half == 0 else NB
            pieces[i, j, half] = (at, rows)
            at += rows
    return at, pieces


ALLROWS, PIECES = place_pieces()
GROWS = ALLROWS // NCHIP
PROWS = 32
ANY = pl.BlockSpec(memory_space=pl.ANY)
F32 = jnp.float32
BF16 = jnp.bfloat16
NT = (((1,), (1,)), ((), ()))
NN = (((1,), (0,)), ((), ()))


def bf16(*shape):
    return jax.ShapeDtypeStruct(shape, BF16)


def f32(*shape):
    return jax.ShapeDtypeStruct(shape, F32)


def split(value):
    high = value.astype(BF16)
    return high, (value - high.astype(F32)).astype(BF16)


def dot3(a, b, dims):
    def one(x, y):
        return lax.dot_general(x, y, dims, preferred_element_type=F32)

    return one(a[0], b[0]) + (one(a[0], b[1]) + one(a[1], b[0]))


def cut_eigenvectors(after_ref, e_ref, out_ref):
    for core in range(2):
        for c in range(NCOL):
            for t in range(4):
                for k in range(8):
                    at = (((k * 2 + core) * NCOL + c) * 4 + t) * 128
                    out_ref[k * NCOL + c, core, t * 4 : t * 4 + 4, :] = e_ref[:, at : at + 128]


def cut_vectors(w_ref, out_ref, done):
    copies = [
        pltpu.make_async_copy(w_ref.at[:, :, c * 512 : c * 512 + 512], out_ref.at[c], done.at[c])
        for c in range(NCOL)
    ]
    for copy in copies:
        copy.start()
    for copy in copies:
        copy.wait()


def split_block(own_ref, sib_ref):
    high, low = [], []
    for ref in (own_ref, sib_ref):
        pair = split(ref[...].reshape(NB, 512))
        high.append(pair[0])
        low.append(pair[1])
    return jnp.concatenate(high, axis=1), jnp.concatenate(low, axis=1)


def inner_products(core_ref, own_ref, sib_ref, buf_ref, high_ref, low_ref):
    def block(j):
        high_ref[j], low_ref[j] = split_block(own_ref, sib_ref)
        for i in range(j + 1):
            value = dot3((high_ref[i], low_ref[i]), (high_ref[j], low_ref[j]), NT)
            for half in range(2):
                at, rows = PIECES[i, j, half]
                buf_ref[at : at + rows, :] = value[:rows, half * 128 : half * 128 + 128]

    for j in range(GROUP):
        pl.when(pl.program_id(0) == j)(lambda j=j: block(j))


def gather_rows(ref, step, first, high_ref, low_ref, value_ref=None, columns=8):
    for t in range(columns):
        for i in range(4):
            value = ref[pl.ds(first + t * 4 + i, NCHIP, stride=step), :]
            high, low = split(value)
            high_ref[i * 64 : i * 64 + 64, t * 128 : t * 128 + 128] = high
            low_ref[i * 64 : i * 64 + 64, t * 128 : t * 128 + 128] = low
            if value_ref is not None:
                value_ref[i * 64 : i * 64 + 64, t * 128 : t * 128 + 128] = value


def scatter_rows(value, block, buf_ref):
    for half in range(2):
        for i in range(4):
            start = (block * 2 + half) * 4 + i
            buf_ref[pl.ds(start, NCHIP, stride=PROWS), :] = value[
                i * 64 : i * 64 + 64, half * 128 : half * 128 + 128
            ]


def local_products(
    core_ref, own_ref, sib_ref, e_ref,
    high_ref, low_ref, x_ref, buf_ref, first_ref, ch_ref, cl_ref,
    eh_ref, el_ref, bh_ref, bl_ref,
):
    core, n = core_ref[0], pl.program_id(0)

    @pl.when(n == 0)
    def _():
        for part in range(2):
            held = core if part == 0 else 1 - core
            at = pl.ds(part * 512, 512)
            gather_rows(
                e_ref, 32, held * 16, eh_ref.at[:, at], el_ref.at[:, at], x_ref.at[:, at], columns=4
            )

    high, low = split_block(own_ref, sib_ref)
    high_ref[0], low_ref[0] = high, low
    value = dot3((eh_ref[...], el_ref[...]), (high, low), NT)

    @pl.when(n < GROUP)
    def _():
        bh_ref[pl.ds(n * NB, NB), :] = high
        bl_ref[pl.ds(n * NB, NB), :] = low
        scatter_rows(value, n, buf_ref)

    @pl.when(n >= GROUP)
    def _():
        first_ref[...] = value
        for j in range(GROUP):
            rows = slice(j * NB, j * NB + NB)
            ch_ref[rows, :], cl_ref[rows, :] = split(
                dot3((bh_ref[rows, :], bl_ref[rows, :]), (high, low), NT)
            )


def sum_chips(buf_ref, rows):
    def add(q, total):
        return total + buf_ref[q]

    return lax.fori_loop(0, NCHIP, add, jnp.zeros((rows, 128), F32), unroll=8)


def spread_to_chips(part, out_ref):
    def spread(q, carry):
        out_ref[q] = part
        return carry

    lax.fori_loop(0, NCHIP, spread, 0, unroll=8)


def sum_products(buf_ref, out_ref):
    spread_to_chips(sum_chips(buf_ref, GROWS), out_ref)


def block_of(g_ref, i, j):
    halves = []
    for half in range(2):
        at, rows = PIECES[i, j, half]
        value = g_ref[at : at + rows, :]
        if rows < NB:
            value = jnp.concatenate([value, jnp.zeros((NB - rows, 128), F32)], axis=0)
        halves.append(value)
    return jnp.concatenate(halves, axis=1)


def invert(g_ref, out_ref):
    row = lax.broadcasted_iota(jnp.int32, (NB, NB), 0)
    col = lax.broadcasted_iota(jnp.int32, (NB, NB), 1)
    apart = row ^ col
    for index, (i, j) in enumerate(PAIRS):
        value = block_of(g_ref, i, j)
        if i == j:
            diagonal = jnp.where(row == col, 0.5 * value, 0.0)
            down = 1.0 / jnp.sum(diagonal, axis=1, keepdims=True)
            across = 1.0 / jnp.sum(diagonal, axis=0, keepdims=True)
            beside = jnp.where((apart == 1) & (row < col), value, 0.0)
            value = jnp.where(row == col, down, 0.0) - down * beside * across
        out_ref[index] = value
    size = 2
    while size < NB:
        for i in range(GROUP):
            index = PAIRS.index((i, i))
            beside = jnp.where((apart >= size) & (apart < 2 * size) & (row < col), block_of(g_ref, i, i), 0.0)
            value = out_ref[index]
            halves = split(value)
            product = dot3(split(dot3(halves, split(beside), NN)), halves, NN)
            out_ref[index] = value - product
        size *= 2


def split_factors(core_ref, own_ref, sib_ref, bh_ref, bl_ref, ah_ref, al_ref):
    mine = core_ref[0] == 0
    bh_ref[...], bl_ref[...] = split(jnp.where(mine, own_ref[...], sib_ref[...]))
    ah_ref[...], al_ref[...] = split(jnp.where(mine, sib_ref[...], own_ref[...]))


def solve(buf_ref, high_ref, low_ref, out_ref, c_ref):
    c_ref[...] = sum_chips(buf_ref, PROWS)

    def factor(i, j):
        index = PAIRS.index((i, j))
        return high_ref[index], low_ref[index]

    found = {}
    for b in range(GROUP - 1, -1, -1):
        rest = jnp.concatenate([c_ref[b * 8 : b * 8 + 4, :], c_ref[b * 8 + 4 : b * 8 + 8, :]], axis=1)
        rest = jnp.concatenate([rest, rest], axis=0)
        for later in range(GROUP - 1, b, -1):
            rest = rest - dot3(found[later], factor(b, later), NT)
        value = dot3(split(rest), factor(b, b), NT)
        found[b] = split(value)
        for half in range(2):
            c_ref[b * 8 + half * 4 : b * 8 + half * 4 + 4, :] = value[0:4, half * 128 : half * 128 + 128]
    spread_to_chips(c_ref[...], out_ref)


def correct_projection(c_ref, gh_ref, gl_ref, first_ref, buf_ref, ch_ref, cl_ref):
    n = pl.program_id(0)

    @pl.when(n == 0)
    def _():
        gather_rows(c_ref, PROWS, 0, ch_ref, cl_ref)

    value = first_ref[...] - dot3((ch_ref[...], cl_ref[...]), (gh_ref[...], gl_ref[...]), NN)
    scatter_rows(value, n, buf_ref)


def updated(c_ref, high_ref, low_ref, x_ref, ch_ref, cl_ref):
    @pl.when(pl.program_id(0) == 0)
    def _():
        gather_rows(c_ref, PROWS, 0, ch_ref, cl_ref)

    vectors = (high_ref[...].reshape(1024, 256), low_ref[...].reshape(1024, 256))
    return x_ref[...] - dot3((ch_ref[...], cl_ref[...]), vectors, NN)


def update(c_ref, high_ref, low_ref, x_ref, out_ref, ch_ref, cl_ref):
    out_ref[...] = updated(c_ref, high_ref, low_ref, x_ref, ch_ref, cl_ref)


def update_last(core_ref, c_ref, high_ref, low_ref, x_ref, out_ref, ch_ref, cl_ref):
    value = updated(c_ref, high_ref, low_ref, x_ref, ch_ref, cl_ref)
    for c in range(NCOL):
        for i in range(4):
            out_ref[c, i * 8 : i * 8 + 8, :] = value[i * 64 + c * 8 : i * 64 + c * 8 + 8, :]


def pass_on(after_ref, in_ref, out_ref):
    pass


def place_rows(in_ref, out_ref, held_ref):
    for c in range(NCOL):
        for t in range(4):
            at = c * 512 + t * 128
            for core in range(2):
                for i in range(4):
                    held_ref[pl.ds((c * 4 + t) * 64 + core * 32 + i, 8, stride=4), :] = in_ref[
                        core * NCOL + c, i * 8 : i * 8 + 8, t * 128 : t * 128 + 128
                    ]
            out_ref[:, at : at + 128] = held_ref[(c * 4 + t) * 64 : (c * 4 + t) * 64 + 64, :]


def whole(*shape):
    return pl.BlockSpec(shape, lambda *_: (0,) * len(shape))


def run(kernel, out_shape, out_specs, in_specs, operands, grid=(1,), scratch=(), core=None, flops=0, size=0, **options):
    spec = pltpu.PrefetchScalarGridSpec(
        num_scalar_prefetch=0 if core is None else 1,
        grid=grid,
        in_specs=in_specs,
        out_specs=out_specs,
        scratch_shapes=list(scratch),
    )
    built = pl.pallas_call(
        kernel,
        out_shape=out_shape,
        grid_spec=spec,
        compiler_params=pltpu.CompilerParams(vmem_limit_bytes=48 * 1024 * 1024),
        cost_estimate=pl.CostEstimate(flops=flops, bytes_accessed=size, transcendentals=0),
        **options,
    )
    return built(*operands) if core is None else built(core, *operands)


def exchange(value, axes):
    return lax.all_to_all(value, axes, 0, 0, tiled=True)


def on_device(eigenvectors, reflectors):
    core = lax.axis_index("core").astype(jnp.int32).reshape(1)
    mega = 2**20
    rows_pair = [pltpu.VMEM((256, 1024), BF16)] * 2

    vectors = run(
        cut_vectors,
        f32(NCOL, 8, 32, 512),
        ANY,
        [ANY],
        (reflectors,),
        scratch=[pltpu.SemaphoreType.DMA((NCOL,))],
        size=8 * mega,
    )
    own = exchange(vectors, COLS)
    sib = lax.ppermute(own, "core", SWAP)
    pieces = run(
        cut_eigenvectors,
        f32(NCHIP, 2, 16, 128),
        whole(NCHIP, 2, 16, 128),
        [ANY, whole(4, 65536)],
        (own, eigenvectors),
        size=2 * mega,
    )
    spread = exchange(pieces, CHIPS).reshape(NCHIP * 32, 128)

    picked = pl.BlockSpec((NCOL, 1, 32, 512), lambda b, core: (0, (1 - core[0]) * GROUP + b, 0, 0))
    buf = run(
        inner_products,
        f32(ALLROWS, 128),
        whole(ALLROWS, 128),
        [picked, picked],
        (own, sib),
        grid=(GROUP,),
        scratch=[pltpu.VMEM((GROUP, NB, 1024), BF16)] * 2,
        core=core,
        flops=4 * 10**9,
        size=6 * mega,
    )

    def after(earlier, value):
        return run(
            pass_on, jax.ShapeDtypeStruct(value.shape, F32), ANY, [ANY, ANY], (earlier, value), input_output_aliases={1: 0}
        )

    buf = after(spread, buf)
    arrived = exchange(buf.reshape(NCHIP, GROWS, 128), CHIPS)

    block = pl.BlockSpec((NCOL, 1, 32, 512), lambda n, core: (0, lax.rem(n + GROUP, 8), 0, 0))
    halves = pl.BlockSpec((1, NB, 1024), lambda n, core: (lax.rem(n + GROUP, 8), 0, 0))
    column = pl.BlockSpec((1024, NB), lambda n, core: (0, jnp.maximum(n - GROUP, 0)))
    high, low, start, buf, first, cross_high, cross_low = run(
        local_products,
        (
            bf16(8, NB, 1024), bf16(8, NB, 1024), f32(256, 1024), f32(NCHIP * PROWS, 128),
            f32(256, 1024), bf16(1024, 1024), bf16(1024, 1024),
        ),
        (
            halves, halves, whole(256, 1024), whole(NCHIP * PROWS, 128),
            pl.BlockSpec((256, NB), lambda n, core: (0, jnp.maximum(n - GROUP, 0))), column, column,
        ),
        [block, block, whole(NCHIP * 32, 128)],
        (own, sib, spread),
        grid=(8,),
        scratch=rows_pair + [pltpu.VMEM((1024, 1024), BF16)] * 2,
        core=core,
        flops=10**10,
        size=24 * mega,
    )
    part = run(
        sum_products,
        f32(NCHIP, GROWS, 128),
        whole(NCHIP, GROWS, 128),
        [whole(NCHIP, GROWS, 128)],
        (arrived,),
        size=5 * mega,
    )
    part = after(first, part)
    gram = exchange(part, CHIPS).reshape(ALLROWS, 128)

    buf = after(gram, buf)
    arrived = exchange(buf.reshape(NCHIP, PROWS, 128), CHIPS)
    count = len(PAIRS)
    factors = run(
        invert,
        f32(count, NB, NB),
        whole(count, NB, NB),
        [whole(ALLROWS, 128)],
        (gram,),
    )
    factors_sib = lax.ppermute(factors, "core", SWAP)
    square = pl.BlockSpec((2, NB, NB), lambda n, core: (n, 0, 0))
    last_high, last_low, first_high, first_low = run(
        split_factors,
        (bf16(count, NB, NB),) * 4,
        (square,) * 4,
        [square, square],
        (factors, factors_sib),
        grid=(count // 2,),
        core=core,
    )

    def coefficients_of(arrived, high, low):
        rows = run(
            solve,
            f32(NCHIP, PROWS, 128),
            whole(NCHIP, PROWS, 128),
            [whole(NCHIP, PROWS, 128), whole(count, NB, NB), whole(count, NB, NB)],
            (arrived, high, low),
            scratch=[pltpu.VMEM((PROWS, 128), F32)],
            flops=10**8,
            size=5 * mega,
        )
        return exchange(rows, CHIPS).reshape(NCHIP * PROWS, 128)

    coefficients = coefficients_of(arrived, last_high, last_low)
    buf = run(
        correct_projection,
        f32(NCHIP * PROWS, 128),
        whole(NCHIP * PROWS, 128),
        [
            whole(NCHIP * PROWS, 128),
            pl.BlockSpec((1024, NB), lambda n: (0, n)),
            pl.BlockSpec((1024, NB), lambda n: (0, n)),
            pl.BlockSpec((256, NB), lambda n: (0, n)),
        ],
        (coefficients, cross_high, cross_low, first),
        grid=(GROUP,),
        scratch=rows_pair,
        flops=2 * 10**9,
        size=7 * mega,
    )
    arrived = exchange(buf.reshape(NCHIP, PROWS, 128), CHIPS)

    def group(which):
        return pl.BlockSpec((GROUP, NB, NB), lambda n, *_: (which, 0, n))

    slab = pl.BlockSpec((256, NB), lambda n, *_: (0, n))
    middle = run(
        update,
        f32(256, 1024),
        slab,
        [whole(NCHIP * PROWS, 128), group(1), group(1), slab],
        (coefficients, high, low, start),
        grid=(4,),
        scratch=rows_pair,
        flops=2 * 10**9,
        size=7 * mega,
    )
    coefficients = coefficients_of(arrived, first_high, first_low)
    finished = run(
        update_last,
        f32(2 * NCOL, 32, 512),
        pl.BlockSpec((NCOL, 32, NB), lambda n, core: (jnp.where(n < 2, core[0], 1 - core[0]), 0, lax.rem(n, 2))),
        [whole(NCHIP * PROWS, 128), group(0), group(0), slab],
        (coefficients, high, low, middle),
        grid=(4,),
        scratch=rows_pair,
        core=core,
        flops=2 * 10**9,
        size=7 * mega,
    )
    return run(
        place_rows,
        f32(64, 4096),
        whole(64, 4096),
        [whole(2 * NCOL, 32, 512)],
        (exchange(finished, CORE_COLS),),
        scratch=[pltpu.VMEM((2048, 128), F32)],
        size=2 * mega,
    )


def solution(mesh):
    fine = Mesh(mesh.devices.reshape(SIZES), AXES)
    in_specs = (P(AXES, None), P(None, COLS, ("y", "xl", "core")))
    out_specs = P(COLS, ("y", "xl", "core"))
    return jax.shard_map(on_device, mesh=fine, in_specs=in_specs, out_specs=out_specs, check_vma=False)
```

```python
import jax
import jax.numpy as jnp
from jax import lax
from jax.experimental import pallas as pl
from jax.experimental.pallas import tpu as pltpu
from jax.sharding import Mesh, PartitionSpec as P

AXES = ("y", "xl", "core", "z", "xh")
SIZES = (4, 2, 2, 4, 2)
CHIPS = ("y", "xl", "z", "xh")
COLS = ("z", "xh")
CORE_COLS = ("core", "z", "xh")
SWAP = ((0, 1), (1, 0))

NCHIP = 64
NCOL = 8
NB = 256
GROUP = 4
PAIRS = [(i, j) for i in range(GROUP) for j in range(i, GROUP)]


def place_pieces():
    at, pieces = 0, {}
    for i, j in PAIRS:
        for half in range(2):
            rows = NB // 2 if i == j and half == 0 else NB
            pieces[i, j, half] = (at, rows)
            at += rows
    return at, pieces


ALLROWS, PIECES = place_pieces()
GROWS = ALLROWS // NCHIP
EROWS = 32
STEP = GROWS + EROWS
PROWS = 32
ANY = pl.BlockSpec(memory_space=pl.ANY)
HBM = pl.BlockSpec(memory_space=pltpu.HBM)
F32 = jnp.float32
BF16 = jnp.bfloat16
NT = (((1,), (1,)), ((), ()))
NN = (((1,), (0,)), ((), ()))


def bf16(*shape):
    return jax.ShapeDtypeStruct(shape, BF16)


def f32(*shape):
    return jax.ShapeDtypeStruct(shape, F32)


def hbm(dtype, *shape):
    return pltpu.HBM(shape, dtype)


def split(value):
    high = value.astype(BF16)
    return high, (value - high.astype(F32)).astype(BF16)


def dot3(a, b, dims):
    def one(x, y):
        return lax.dot_general(x, y, dims, preferred_element_type=F32)

    return one(a[0], b[0]) + (one(a[0], b[1]) + one(a[1], b[0]))


def cut_eigenvectors(e_ref, out_ref):
    for core in range(2):
        for c in range(NCOL):
            for t in range(4):
                for k in range(8):
                    at = (((k * 2 + core) * NCOL + c) * 4 + t) * 128
                    out_ref[k * NCOL + c, core * 16 + t * 4 : core * 16 + t * 4 + 4, :] = e_ref[:, at : at + 128]


def cut_vectors(w_ref, out_ref, done):
    copies = []
    for core in range(2):
        for c in range(NCOL):
            to = core * NCOL + c
            first = (1 - core) * GROUP
            copies.append(
                pltpu.make_async_copy(
                    w_ref.at[first : first + GROUP, :, c * 512 : c * 512 + 512], out_ref.at[to], done.at[to]
                )
            )
    for copy in copies:
        copy.start()
    for copy in copies:
        copy.wait()


def whole_block(value):
    return jnp.concatenate([value[:NCOL].reshape(NB, 512), value[NCOL:].reshape(NB, 512)], axis=1)


def inner_products(w_ref, e_ref, buf_ref, high_ref, low_ref):
    def block(j):
        high_ref[j], low_ref[j] = split(whole_block(w_ref[:, 0]))
        for i in range(j + 1):
            value = dot3((high_ref[i], low_ref[i]), (high_ref[j], low_ref[j]), NT)
            for half in range(2):
                at, rows = PIECES[i, j, half]
                done = 0
                while done < rows:
                    chip, offset = divmod(at + done, GROWS)
                    take = min(rows - done, GROWS - offset)
                    start = chip * STEP + offset
                    buf_ref[start : start + take, :] = value[done : done + take, half * 128 : half * 128 + 128]
                    done += take

    for j in range(GROUP):
        pl.when(pl.program_id(0) == j)(lambda j=j: block(j))

    @pl.when(pl.program_id(0) == 0)
    def _():
        for q in range(NCHIP):
            buf_ref[q * STEP + GROWS : q * STEP + STEP, :] = e_ref[q]


def gather_rows(ref, step, first, high_ref, low_ref, value_ref=None, columns=8):
    for t in range(columns):
        for i in range(4):
            value = ref[pl.ds(first + t * 4 + i, NCHIP, stride=step), :]
            high, low = split(value)
            high_ref[i * 64 : i * 64 + 64, t * 128 : t * 128 + 128] = high
            low_ref[i * 64 : i * 64 + 64, t * 128 : t * 128 + 128] = low
            if value_ref is not None:
                value_ref[i * 64 : i * 64 + 64, t * 128 : t * 128 + 128] = value


def scatter_rows(value, block, buf_ref):
    for half in range(2):
        for i in range(4):
            start = (block * 2 + half) * 4 + i
            buf_ref[pl.ds(start, NCHIP, stride=PROWS), :] = value[
                i * 64 : i * 64 + 64, half * 128 : half * 128 + 128
            ]


def local_products(
    core_ref, mine_ref, other_ref, e_ref,
    high_ref, low_ref, x_ref, buf_ref, first_ref, ch_ref, cl_ref,
    eh_ref, el_ref, bh_ref, bl_ref,
):
    core, n = core_ref[0], pl.program_id(0)

    @pl.when(n == 0)
    def _():
        for part in range(2):
            at = pl.ds(part * 512, 512)
            gather_rows(
                e_ref, EROWS, part * 16, eh_ref.at[:, at], el_ref.at[:, at], x_ref.at[:, at], columns=4
            )

    held = (core == 0) == (n < GROUP)
    high, low = split(jnp.where(held, whole_block(mine_ref[:, 0]), whole_block(other_ref[:, 0])))
    high_ref[0], low_ref[0] = high, low
    value = dot3((eh_ref[...], el_ref[...]), (high, low), NT)

    @pl.when(n < GROUP)
    def _():
        bh_ref[pl.ds(n * NB, NB), :] = high
        bl_ref[pl.ds(n * NB, NB), :] = low
        scatter_rows(value, n, buf_ref)

    @pl.when(n >= GROUP)
    def _():
        first_ref[...] = value
        for j in range(GROUP):
            rows = slice(j * NB, j * NB + NB)
            ch_ref[rows, :], cl_ref[rows, :] = split(
                dot3((bh_ref[rows, :], bl_ref[rows, :]), (high, low), NT)
            )


def sum_chips(buf_ref, rows):
    def add(q, total):
        return total + buf_ref[q, :rows, :]

    return lax.fori_loop(0, NCHIP, add, jnp.zeros((rows, 128), F32), unroll=8)


def sum_projection(buf_ref, out_ref):
    out_ref[...] = sum_chips(buf_ref, PROWS)


def spread_to_chips(part_ref, out_ref, done, beside=None):
    copies = [pltpu.make_async_copy(part_ref, out_ref.at[q], done.at[q]) for q in range(NCHIP)]
    for copy in copies:
        copy.start()
    if beside is not None:
        beside()
    for copy in copies:
        copy.wait()


def spread_rows(part, out_ref):
    def spread(q, carry):
        out_ref[q] = part
        return carry

    lax.fori_loop(0, NCHIP, spread, 0, unroll=8)


def sum_products(buf_ref, out_ref, e_ref, part_ref, done):
    part_ref[...] = sum_chips(buf_ref, GROWS)

    def keep_eigenvectors():
        e_ref[...] = buf_ref[:, GROWS:, :]

    spread_to_chips(part_ref, out_ref, done, keep_eigenvectors)


def spread_found(core_ref, own_ref, sib_ref, out_ref):
    spread_rows(jnp.where(core_ref[0] == 0, own_ref[...], sib_ref[...]), out_ref)


def block_of(g_ref, i, j):
    halves = []
    for half in range(2):
        at, rows = PIECES[i, j, half]
        value = g_ref[at : at + rows, :]
        if rows < NB:
            value = jnp.concatenate([value, jnp.zeros((NB - rows, 128), F32)], axis=0)
        halves.append(value)
    return jnp.concatenate(halves, axis=1)


def invert(g_ref, out_ref, high_ref, low_ref):
    row = lax.broadcasted_iota(jnp.int32, (NB, NB), 0)
    col = lax.broadcasted_iota(jnp.int32, (NB, NB), 1)
    apart = row ^ col
    for index, (i, j) in enumerate(PAIRS):
        value = block_of(g_ref, i, j)
        if i == j:
            diagonal = jnp.where(row == col, 0.5 * value, 0.0)
            down = 1.0 / jnp.sum(diagonal, axis=1, keepdims=True)
            across = 1.0 / jnp.sum(diagonal, axis=0, keepdims=True)
            beside = jnp.where((apart == 1) & (row < col), value, 0.0)
            value = jnp.where(row == col, down, 0.0) - down * beside * across
        out_ref[index] = value
    size = 2
    while size < NB:
        for i in range(GROUP):
            index = PAIRS.index((i, i))
            beside = jnp.where((apart >= size) & (apart < 2 * size) & (row < col), block_of(g_ref, i, i), 0.0)
            value = out_ref[index]
            halves = split(value)
            product = dot3(split(dot3(halves, split(beside), NN)), halves, NN)
            out_ref[index] = value - product
        size *= 2
    for index in range(len(PAIRS)):
        high_ref[index], low_ref[index] = split(out_ref[index])


def pick_factors(core_ref, own_ref, sib_ref, high_ref, low_ref):
    high_ref[...], low_ref[...] = split(jnp.where(core_ref[0] == 1, own_ref[...], sib_ref[...]))


def solve(rows_of, high_ref, low_ref, keep):
    def factor(i, j):
        index = PAIRS.index((i, j))
        return high_ref[index], low_ref[index]

    found = {}
    for b in range(GROUP - 1, -1, -1):
        rest = jnp.concatenate([rows_of(b * 2), rows_of(b * 2 + 1)], axis=1)
        for later in range(GROUP - 1, b, -1):
            rest = rest - dot3(found[later], factor(b, later), NT)
        value = dot3(split(rest), factor(b, b), NT)
        found[b] = split(value)
        for half in range(2):
            keep(b * 2 + half, value[:, half * 128 : half * 128 + 128])


def solve_both(own_ref, sib_ref, high_ref, low_ref, c_own_ref, c_sib_ref):
    def rows_of(t):
        return jnp.concatenate([own_ref[t * 4 : t * 4 + 4, :], sib_ref[t * 4 : t * 4 + 4, :]], axis=0)

    def keep(t, value):
        c_own_ref[t * 4 : t * 4 + 4, :] = value[0:4]
        c_sib_ref[t * 4 : t * 4 + 4, :] = value[4:8]

    solve(rows_of, high_ref, low_ref, keep)


def solve_own(buf_ref, high_ref, low_ref, out_ref, c_ref):
    c_ref[...] = sum_chips(buf_ref, PROWS)

    def rows_of(t):
        return jnp.concatenate([c_ref[t * 4 : t * 4 + 4, :]] * 2, axis=0)

    def keep(t, value):
        c_ref[t * 4 : t * 4 + 4, :] = value[0:4]

    solve(rows_of, high_ref, low_ref, keep)
    spread_rows(c_ref[...], out_ref)


def correct_projection(c_ref, gh_ref, gl_ref, first_ref, buf_ref, ch_ref, cl_ref):
    n = pl.program_id(0)

    @pl.when(n == 0)
    def _():
        gather_rows(c_ref, PROWS, 0, ch_ref, cl_ref)

    value = first_ref[...] - dot3((ch_ref[...], cl_ref[...]), (gh_ref[...], gl_ref[...]), NN)
    scatter_rows(value, n, buf_ref)


def updated(c_ref, high_ref, low_ref, x_ref, ch_ref, cl_ref):
    @pl.when(pl.program_id(0) == 0)
    def _():
        gather_rows(c_ref, PROWS, 0, ch_ref, cl_ref)

    vectors = (high_ref[...].reshape(1024, 256), low_ref[...].reshape(1024, 256))
    return x_ref[...] - dot3((ch_ref[...], cl_ref[...]), vectors, NN)


def update(c_ref, high_ref, low_ref, x_ref, out_ref, ch_ref, cl_ref):
    out_ref[...] = updated(c_ref, high_ref, low_ref, x_ref, ch_ref, cl_ref)


def update_last(c_ref, high_ref, low_ref, x_ref, out_ref, ch_ref, cl_ref):
    value = updated(c_ref, high_ref, low_ref, x_ref, ch_ref, cl_ref)
    for c in range(NCOL):
        for i in range(4):
            out_ref[c, i * 8 : i * 8 + 8, :] = value[i * 64 + c * 8 : i * 64 + c * 8 + 8, :]


def pass_on(after_ref, in_ref, out_ref):
    pass


def place_rows(in_ref, out_ref, held_ref):
    for c in range(NCOL):
        for t in range(4):
            at = c * 512 + t * 128
            for core in range(2):
                for i in range(4):
                    held_ref[pl.ds((c * 4 + t) * 64 + core * 32 + i, 8, stride=4), :] = in_ref[
                        core * NCOL + c, i * 8 : i * 8 + 8, t * 128 : t * 128 + 128
                    ]
            out_ref[:, at : at + 128] = held_ref[(c * 4 + t) * 64 : (c * 4 + t) * 64 + 64, :]


def whole(*shape):
    return pl.BlockSpec(shape, lambda *_: (0,) * len(shape))


def run(kernel, out_shape, out_specs, in_specs, operands, grid=(1,), scratch=(), core=None, flops=0, size=0, limit=40, pin=(), **options):
    operands = [in_hbm(value) if at in pin else value for at, value in enumerate(operands)]
    spec = pltpu.PrefetchScalarGridSpec(
        num_scalar_prefetch=0 if core is None else 1,
        grid=grid,
        in_specs=in_specs,
        out_specs=out_specs,
        scratch_shapes=list(scratch),
    )
    built = pl.pallas_call(
        kernel,
        out_shape=out_shape,
        grid_spec=spec,
        compiler_params=pltpu.CompilerParams(vmem_limit_bytes=limit * 2**20),
        cost_estimate=pl.CostEstimate(flops=flops, bytes_accessed=size, transcendentals=0),
        **options,
    )
    return built(*operands) if core is None else built(core, *operands)


def in_hbm(value):
    return pltpu.with_memory_space_constraint(value, pltpu.HBM)


def exchange(value, axes):
    return lax.all_to_all(value, axes, 0, 0, tiled=True)


def on_device(eigenvectors, reflectors):
    core = lax.axis_index("core").astype(jnp.int32).reshape(1)
    mega = 2**20
    rows_pair = [pltpu.VMEM((256, 1024), BF16)] * 2

    def after(earlier, value, pin=(0,)):
        return run(
            pass_on, jax.ShapeDtypeStruct(value.shape, F32), ANY, [ANY, ANY], (earlier, value), pin=pin, input_output_aliases={1: 0}
        )

    vectors = run(
        cut_vectors,
        f32(2 * NCOL, GROUP, 32, 512),
        whole(2 * NCOL, GROUP, 32, 512),
        [HBM],
        (reflectors,),
        pin=(0,),
        scratch=[pltpu.SemaphoreType.DMA((2 * NCOL,))],
        size=8 * mega,
    )
    mine = exchange(vectors, CORE_COLS)
    other = lax.ppermute(mine, "core", SWAP)
    pieces = run(
        cut_eigenvectors, f32(NCHIP, EROWS, 128), whole(NCHIP, EROWS, 128), [whole(4, 65536)], (eigenvectors,), size=2 * mega
    )
    buf = run(
        inner_products,
        f32(NCHIP * STEP, 128),
        whole(NCHIP * STEP, 128),
        [pl.BlockSpec((2 * NCOL, 1, 32, 512), lambda b: (0, b, 0, 0)), whole(NCHIP, EROWS, 128)],
        (mine, pieces),
        grid=(GROUP,),
        scratch=[pltpu.VMEM((GROUP, NB, 1024), BF16)] * 2,
        flops=4 * 10**9,
        size=6 * mega,
    )
    arrived = exchange(after(other, buf).reshape(NCHIP, STEP, 128), CHIPS)

    part, spread = run(
        sum_products,
        (hbm(F32, NCHIP, GROWS, 128), f32(NCHIP, EROWS, 128)),
        (HBM, whole(NCHIP, EROWS, 128)),
        [whole(NCHIP, STEP, 128)],
        (arrived,),
        scratch=[pltpu.VMEM((GROWS, 128), F32), pltpu.SemaphoreType.DMA((NCHIP,))],
        size=5 * mega,
    )

    block = pl.BlockSpec((2 * NCOL, 1, 32, 512), lambda n, core: (0, lax.rem(n, GROUP), 0, 0))
    halves = pl.BlockSpec((1, NB, 1024), lambda n, core: (lax.rem(n + GROUP, 8), 0, 0))
    column = pl.BlockSpec((1024, NB), lambda n, core: (0, jnp.maximum(n - GROUP, 0)))
    high, low, start, buf, first, cross_high, cross_low = run(
        local_products,
        (
            hbm(BF16, 8, NB, 1024), hbm(BF16, 8, NB, 1024), hbm(F32, 256, 1024), hbm(F32, NCHIP * PROWS, 128),
            hbm(F32, 256, 1024), hbm(BF16, 1024, 1024), hbm(BF16, 1024, 1024),
        ),
        (
            halves, halves, whole(256, 1024), whole(NCHIP * PROWS, 128),
            pl.BlockSpec((256, NB), lambda n, core: (0, jnp.maximum(n - GROUP, 0))), column, column,
        ),
        [block, block, whole(NCHIP * EROWS, 128)],
        (mine, other, spread.reshape(NCHIP * EROWS, 128)),
        pin=(0, 1),
        grid=(8,),
        scratch=rows_pair + [pltpu.VMEM((1024, 1024), BF16)] * 2,
        core=core,
        flops=10**10,
        size=24 * mega,
    )
    gram = after(first, exchange(part, CHIPS)).reshape(ALLROWS, 128)

    count = len(PAIRS)
    factors, own_high, own_low = run(
        invert,
        (hbm(F32, count, NB, NB), bf16(count, NB, NB), bf16(count, NB, NB)),
        (whole(count, NB, NB),) * 3,
        [whole(ALLROWS, 128)],
        (gram,),
    )
    arrived = after(factors, exchange(after(gram, buf, (1,)).reshape(NCHIP, PROWS, 128), CHIPS))
    rows = f32(PROWS, 128)
    projection = run(sum_projection, rows, whole(PROWS, 128), [whole(NCHIP, PROWS, 128)], (arrived,), size=mega)
    found, found_sib = run(
        solve_both,
        (rows, rows),
        (whole(PROWS, 128),) * 2,
        [whole(PROWS, 128), whole(PROWS, 128), whole(count, NB, NB), whole(count, NB, NB)],
        (projection, lax.ppermute(projection, "core", SWAP), own_high, own_low),
        flops=10**8,
        size=3 * mega,
    )
    found = run(
        spread_found,
        f32(NCHIP, PROWS, 128),
        whole(NCHIP, PROWS, 128),
        [whole(PROWS, 128), whole(PROWS, 128)],
        (found, lax.ppermute(found_sib, "core", SWAP)),
        core=core,
        size=mega,
    )
    coefficients = exchange(found, CHIPS)
    factors = after(coefficients, factors, (1,))
    coefficients = coefficients.reshape(NCHIP * PROWS, 128)
    square = pl.BlockSpec((2, NB, NB), lambda n, core: (n, 0, 0))
    first_high, first_low = run(
        pick_factors,
        (hbm(BF16, count, NB, NB),) * 2,
        (square,) * 2,
        [square, square],
        (factors, lax.ppermute(factors, "core", SWAP)),
        grid=(count // 2,),
        core=core,
        size=8 * mega,
    )
    buf = run(
        correct_projection,
        f32(NCHIP * PROWS, 128),
        whole(NCHIP * PROWS, 128),
        [
            whole(NCHIP * PROWS, 128),
            pl.BlockSpec((1024, NB), lambda n: (0, n)),
            pl.BlockSpec((1024, NB), lambda n: (0, n)),
            pl.BlockSpec((256, NB), lambda n: (0, n)),
        ],
        (coefficients, cross_high, cross_low, first),
        pin=(1, 2, 3),
        grid=(GROUP,),
        scratch=rows_pair,
        flops=2 * 10**9,
        size=7 * mega,
    )

    def group(which):
        return pl.BlockSpec((GROUP, NB, NB), lambda n, *_: (which, 0, n))

    slab = pl.BlockSpec((256, NB), lambda n, *_: (0, n))
    middle = run(
        update,
        f32(256, 1024),
        slab,
        [whole(NCHIP * PROWS, 128), group(1), group(1), slab],
        (coefficients, high, low, start),
        pin=(1, 2, 3),
        grid=(4,),
        scratch=rows_pair,
        flops=2 * 10**9,
        size=7 * mega,
    )
    arrived = after(middle, after(first_high, exchange(buf.reshape(NCHIP, PROWS, 128), CHIPS)), ())
    found = run(
        solve_own,
        f32(NCHIP, PROWS, 128),
        whole(NCHIP, PROWS, 128),
        [whole(NCHIP, PROWS, 128), whole(count, NB, NB), whole(count, NB, NB)],
        (arrived, first_high, first_low),
        scratch=[pltpu.VMEM((PROWS, 128), F32)],
        flops=10**8,
        size=5 * mega,
    )
    coefficients = exchange(found, CHIPS).reshape(NCHIP * PROWS, 128)
    finished = run(
        update_last,
        f32(2 * NCOL, 32, 512),
        pl.BlockSpec((NCOL, 32, NB), lambda n: (n // 2, 0, lax.rem(n, 2))),
        [whole(NCHIP * PROWS, 128), group(0), group(0), slab],
        (coefficients, high, low, middle),
        pin=(1, 2),
        grid=(4,),
        scratch=rows_pair,
        flops=2 * 10**9,
        size=7 * mega,
    )
    return run(
        place_rows,
        f32(64, 4096),
        whole(64, 4096),
        [whole(2 * NCOL, 32, 512)],
        (exchange(finished, CORE_COLS),),
        scratch=[pltpu.VMEM((2048, 128), F32)],
        size=2 * mega,
    )


def solution(mesh):
    fine = Mesh(mesh.devices.reshape(SIZES), AXES)
    in_specs = (P(AXES, None), P(None, COLS, ("y", "xl", "core")))
    out_specs = P(COLS, ("y", "xl", "core"))
    return jax.shard_map(on_device, mesh=fine, in_specs=in_specs, out_specs=out_specs, check_vma=False)
```

```python
import jax
import jax.numpy as jnp
from jax import lax
from jax.experimental import pallas as pl
from jax.experimental.pallas import tpu as pltpu
from jax.sharding import Mesh, PartitionSpec as P

AXES = ("y", "xl", "core", "z", "xh")
SIZES = (4, 2, 2, 4, 2)
CHIPS = ("y", "xl", "z", "xh")
COLS = ("z", "xh")
CORE_COLS = ("core", "z", "xh")
SWAP = ((0, 1), (1, 0))

NCHIP = 64
NCOL = 8
NB = 256
GROUP = 4
PAIRS = [(i, j) for i in range(GROUP) for j in range(i, GROUP)]


def place_pieces():
    at, pieces = 0, {}
    for i, j in PAIRS:
        for half in range(2):
            rows = NB // 2 if i == j and half == 0 else NB
            pieces[i, j, half] = (at, rows)
            at += rows
    return at, pieces


ALLROWS, PIECES = place_pieces()
GROWS = ALLROWS // NCHIP
EROWS = 32
STEP = GROWS + EROWS
PROWS = 32
ANY = pl.BlockSpec(memory_space=pl.ANY)
HBM = pl.BlockSpec(memory_space=pltpu.HBM)
VMEM = pl.BlockSpec(memory_space=pltpu.VMEM)
F32 = jnp.float32
BF16 = jnp.bfloat16
NT = (((1,), (1,)), ((), ()))
NN = (((1,), (0,)), ((), ()))


def bf16(*shape):
    return jax.ShapeDtypeStruct(shape, BF16)


def f32(*shape):
    return jax.ShapeDtypeStruct(shape, F32)


def hbm(dtype, *shape):
    return pltpu.HBM(shape, dtype)


def split(value):
    high = value.astype(BF16)
    return high, (value - high.astype(F32)).astype(BF16)


def dot3(a, b, dims):
    def one(x, y):
        return lax.dot_general(x, y, dims, preferred_element_type=F32)

    return one(a[0], b[0]) + (one(a[0], b[1]) + one(a[1], b[0]))


def cut_eigenvectors(after_ref, e_ref, out_ref):
    for core in range(2):
        for c in range(NCOL):
            for t in range(4):
                for k in range(8):
                    at = (((k * 2 + core) * NCOL + c) * 4 + t) * 128
                    out_ref[k * NCOL + c, core * 16 + t * 4 : core * 16 + t * 4 + 4, :] = e_ref[:, at : at + 128]


def cut_vectors(w_ref, out_ref, done):
    copies = []
    for core in range(2):
        for c in range(NCOL):
            to = core * NCOL + c
            first = (1 - core) * GROUP
            copies.append(
                pltpu.make_async_copy(
                    w_ref.at[first : first + GROUP, :, c * 512 : c * 512 + 512], out_ref.at[to], done.at[to]
                )
            )
    for copy in copies:
        copy.start()
    for copy in copies:
        copy.wait()


def whole_block(value):
    return jnp.concatenate([value[:NCOL].reshape(NB, 512), value[NCOL:].reshape(NB, 512)], axis=1)


def inner_products(w_ref, e_ref, buf_ref, kept_ref, high_ref, low_ref, done):
    keep = pltpu.make_async_copy(w_ref, kept_ref, done)
    keep.start()
    for j in range(GROUP):
        high_ref[j], low_ref[j] = split(whole_block(w_ref[:, j]))
        for i in range(j + 1):
            value = dot3((high_ref[i], low_ref[i]), (high_ref[j], low_ref[j]), NT)
            for half in range(2):
                at, rows = PIECES[i, j, half]
                done = 0
                while done < rows:
                    chip, offset = divmod(at + done, GROWS)
                    take = min(rows - done, GROWS - offset)
                    start = chip * STEP + offset
                    buf_ref[start : start + take, :] = value[done : done + take, half * 128 : half * 128 + 128]
                    done += take
    for q in range(NCHIP):
        buf_ref[q * STEP + GROWS : q * STEP + STEP, :] = e_ref[q]
    keep.wait()


def gather_rows(ref, step, first, high_ref, low_ref, value_ref=None, columns=8):
    for t in range(columns):
        for i in range(4):
            value = ref[pl.ds(first + t * 4 + i, NCHIP, stride=step), :]
            high, low = split(value)
            high_ref[i * 64 : i * 64 + 64, t * 128 : t * 128 + 128] = high
            low_ref[i * 64 : i * 64 + 64, t * 128 : t * 128 + 128] = low
            if value_ref is not None:
                value_ref[i * 64 : i * 64 + 64, t * 128 : t * 128 + 128] = value


def scatter_rows(value, block, buf_ref):
    for half in range(2):
        for i in range(4):
            start = (block * 2 + half) * 4 + i
            buf_ref[pl.ds(start, NCHIP, stride=PROWS), :] = value[
                i * 64 : i * 64 + 64, half * 128 : half * 128 + 128
            ]


def local_products(
    core_ref, mine_ref, other_ref, e_ref,
    high_b_ref, low_b_ref, high_a_ref, low_a_ref, x_ref, buf_ref, first_ref, ch_ref, cl_ref,
    eh_ref, el_ref, bh_ref, bl_ref,
):
    core, n = core_ref[0], pl.program_id(0)

    @pl.when(n == 0)
    def _():
        for part in range(2):
            at = pl.ds(part * 512, 512)
            gather_rows(
                e_ref, EROWS, part * 16, eh_ref.at[:, at], el_ref.at[:, at], x_ref.at[:, at], columns=4
            )

    held = (core == 0) == (n < GROUP)
    high, low = split(jnp.where(held, whole_block(mine_ref[:, 0]), whole_block(other_ref[:, 0])))
    value = dot3((eh_ref[...], el_ref[...]), (high, low), NT)

    @pl.when(n < GROUP)
    def _():
        high_b_ref[0], low_b_ref[0] = high, low
        bh_ref[pl.ds(n * NB, NB), :] = high
        bl_ref[pl.ds(n * NB, NB), :] = low
        scatter_rows(value, n, buf_ref)

    @pl.when(n >= GROUP)
    def _():
        high_a_ref[0], low_a_ref[0] = high, low
        first_ref[...] = value
        for j in range(GROUP):
            rows = slice(j * NB, j * NB + NB)
            ch_ref[rows, :], cl_ref[rows, :] = split(
                dot3((bh_ref[rows, :], bl_ref[rows, :]), (high, low), NT)
            )


def sum_chips(buf_ref, rows):
    def add(q, total):
        return total + buf_ref[q, :rows, :]

    return lax.fori_loop(0, NCHIP, add, jnp.zeros((rows, 128), F32), unroll=8)


def sum_projection(buf_ref, out_ref):
    out_ref[...] = sum_chips(buf_ref, PROWS)


def spread_to_chips(part_ref, out_ref, done, beside=None):
    copies = [pltpu.make_async_copy(part_ref, out_ref.at[q], done.at[q]) for q in range(NCHIP)]
    for copy in copies:
        copy.start()
    if beside is not None:
        beside()
    for copy in copies:
        copy.wait()


def spread_rows(part, out_ref):
    def spread(q, carry):
        out_ref[q] = part
        return carry

    lax.fori_loop(0, NCHIP, spread, 0, unroll=8)


def sum_products(buf_ref, out_ref, e_ref, part_ref, done):
    part_ref[...] = sum_chips(buf_ref, GROWS)

    def keep_eigenvectors():
        e_ref[...] = buf_ref[:, GROWS:, :]

    spread_to_chips(part_ref, out_ref, done, keep_eigenvectors)


def spread_found(core_ref, own_ref, sib_ref, out_ref):
    spread_rows(jnp.where(core_ref[0] == 0, own_ref[...], sib_ref[...]), out_ref)


def block_of(g_ref, i, j):
    halves = []
    for half in range(2):
        at, rows = PIECES[i, j, half]
        value = g_ref[at : at + rows, :]
        if rows < NB:
            value = jnp.concatenate([value, jnp.zeros((NB - rows, 128), F32)], axis=0)
        halves.append(value)
    return jnp.concatenate(halves, axis=1)


def invert(g_ref, out_ref, high_ref, low_ref):
    row = lax.broadcasted_iota(jnp.int32, (NB, NB), 0)
    col = lax.broadcasted_iota(jnp.int32, (NB, NB), 1)
    apart = row ^ col
    for index, (i, j) in enumerate(PAIRS):
        value = block_of(g_ref, i, j)
        if i == j:
            diagonal = jnp.where(row == col, 0.5 * value, 0.0)
            down = 1.0 / jnp.sum(diagonal, axis=1, keepdims=True)
            across = 1.0 / jnp.sum(diagonal, axis=0, keepdims=True)
            beside = jnp.where((apart == 1) & (row < col), value, 0.0)
            value = jnp.where(row == col, down, 0.0) - down * beside * across
        out_ref[index] = value
    size = 2
    while size < NB:
        for i in range(GROUP):
            index = PAIRS.index((i, i))
            beside = jnp.where((apart >= size) & (apart < 2 * size) & (row < col), block_of(g_ref, i, i), 0.0)
            value = out_ref[index]
            halves = split(value)
            product = dot3(split(dot3(halves, split(beside), NN)), halves, NN)
            out_ref[index] = value - product
        size *= 2
    for index in range(len(PAIRS)):
        high_ref[index], low_ref[index] = split(out_ref[index])


def pick_factors(core_ref, own_ref, sib_ref, high_ref, low_ref):
    high_ref[...], low_ref[...] = split(jnp.where(core_ref[0] == 1, own_ref[...], sib_ref[...]))


def solve(rows_of, high_ref, low_ref, keep):
    def factor(i, j):
        index = PAIRS.index((i, j))
        return high_ref[index], low_ref[index]

    found = {}
    for b in range(GROUP - 1, -1, -1):
        rest = jnp.concatenate([rows_of(b * 2), rows_of(b * 2 + 1)], axis=1)
        for later in range(GROUP - 1, b, -1):
            rest = rest - dot3(found[later], factor(b, later), NT)
        value = dot3(split(rest), factor(b, b), NT)
        found[b] = split(value)
        for half in range(2):
            keep(b * 2 + half, value[:, half * 128 : half * 128 + 128])


def solve_both(own_ref, sib_ref, high_ref, low_ref, c_own_ref, c_sib_ref):
    def rows_of(t):
        return jnp.concatenate([own_ref[t * 4 : t * 4 + 4, :], sib_ref[t * 4 : t * 4 + 4, :]], axis=0)

    def keep(t, value):
        c_own_ref[t * 4 : t * 4 + 4, :] = value[0:4]
        c_sib_ref[t * 4 : t * 4 + 4, :] = value[4:8]

    solve(rows_of, high_ref, low_ref, keep)


def solve_own(buf_ref, high_ref, low_ref, out_ref, c_ref):
    c_ref[...] = sum_chips(buf_ref, PROWS)

    def rows_of(t):
        return jnp.concatenate([c_ref[t * 4 : t * 4 + 4, :]] * 2, axis=0)

    def keep(t, value):
        c_ref[t * 4 : t * 4 + 4, :] = value[0:4]

    solve(rows_of, high_ref, low_ref, keep)
    spread_rows(c_ref[...], out_ref)


def correct_projection(c_ref, gh_ref, gl_ref, first_ref, buf_ref, ch_ref, cl_ref):
    gather_rows(c_ref, PROWS, 0, ch_ref, cl_ref)
    for n in range(GROUP):
        at = slice(n * NB, n * NB + NB)
        value = first_ref[:, at] - dot3((ch_ref[...], cl_ref[...]), (gh_ref[:, at], gl_ref[:, at]), NN)
        scatter_rows(value, n, buf_ref)


def updated(n, high_ref, low_ref, x_ref, ch_ref, cl_ref):
    at = slice(n * NB, n * NB + NB)
    vectors = (high_ref[:, :, at].reshape(1024, NB), low_ref[:, :, at].reshape(1024, NB))
    return x_ref[:, at] - dot3((ch_ref[...], cl_ref[...]), vectors, NN)


def update(c_ref, high_ref, low_ref, x_ref, out_ref, ch_ref, cl_ref):
    gather_rows(c_ref, PROWS, 0, ch_ref, cl_ref)
    for n in range(4):
        out_ref[:, n * NB : n * NB + NB] = updated(n, high_ref, low_ref, x_ref, ch_ref, cl_ref)


def update_last(c_ref, high_ref, low_ref, x_ref, out_ref, ch_ref, cl_ref):
    gather_rows(c_ref, PROWS, 0, ch_ref, cl_ref)
    for n in range(4):
        value = updated(n, high_ref, low_ref, x_ref, ch_ref, cl_ref)
        at = n % 2 * NB
        for c in range(NCOL):
            for i in range(4):
                rows = slice(i * 64 + c * 8, i * 64 + c * 8 + 8)
                out_ref[n // 2 * NCOL + c, i * 8 : i * 8 + 8, at : at + NB] = value[rows, :]


def pass_on(after_ref, in_ref, out_ref):
    pass


def place_rows(in_ref, out_ref, held_ref):
    for c in range(NCOL):
        for t in range(4):
            at = c * 512 + t * 128
            for core in range(2):
                for i in range(4):
                    held_ref[pl.ds((c * 4 + t) * 64 + core * 32 + i, 8, stride=4), :] = in_ref[
                        core * NCOL + c, i * 8 : i * 8 + 8, t * 128 : t * 128 + 128
                    ]
            out_ref[:, at : at + 128] = held_ref[(c * 4 + t) * 64 : (c * 4 + t) * 64 + 64, :]


def whole(*shape):
    return pl.BlockSpec(shape, lambda *_: (0,) * len(shape))


def run(kernel, out_shape, out_specs, in_specs, operands, grid=(1,), scratch=(), core=None, flops=0, size=0, limit=32, pin=(), **options):
    operands = [in_hbm(value) if at in pin else value for at, value in enumerate(operands)]
    spec = pltpu.PrefetchScalarGridSpec(
        num_scalar_prefetch=0 if core is None else 1,
        grid=grid,
        in_specs=in_specs,
        out_specs=out_specs,
        scratch_shapes=list(scratch),
    )
    built = pl.pallas_call(
        kernel,
        out_shape=out_shape,
        grid_spec=spec,
        compiler_params=pltpu.CompilerParams(vmem_limit_bytes=limit * 2**20),
        cost_estimate=pl.CostEstimate(flops=flops, bytes_accessed=size, transcendentals=0),
        **options,
    )
    return built(*operands) if core is None else built(core, *operands)


def direct(kernel, out_shape, operands, scratch=(), out_specs=None, flops=0, size=0, limit=32):
    return pl.pallas_call(
        kernel,
        out_shape=out_shape,
        in_specs=[VMEM] * len(operands),
        out_specs=jax.tree.map(lambda _: VMEM, out_shape) if out_specs is None else out_specs,
        scratch_shapes=list(scratch),
        compiler_params=pltpu.CompilerParams(vmem_limit_bytes=limit * 2**20),
        cost_estimate=pl.CostEstimate(flops=flops, bytes_accessed=size, transcendentals=0),
    )(*operands)


def in_hbm(value):
    return pltpu.with_memory_space_constraint(value, pltpu.HBM)


def exchange(value, axes):
    return lax.all_to_all(value, axes, 0, 0, tiled=True)


def on_device(eigenvectors, reflectors):
    core = lax.axis_index("core").astype(jnp.int32).reshape(1)
    mega = 2**20
    rows_pair = [pltpu.VMEM((256, 1024), BF16)] * 2

    def after(earlier, value, pin=(0,)):
        return run(
            pass_on, jax.ShapeDtypeStruct(value.shape, F32), ANY, [ANY, ANY], (earlier, value), pin=pin, size=1024, input_output_aliases={1: 0}
        )

    vectors = run(
        cut_vectors,
        f32(2 * NCOL, GROUP, 32, 512),
        whole(2 * NCOL, GROUP, 32, 512),
        [HBM],
        (reflectors,),
        pin=(0,),
        scratch=[pltpu.SemaphoreType.DMA((2 * NCOL,))],
        size=8 * mega,
    )
    mine = exchange(vectors, CORE_COLS)
    pieces = run(
        cut_eigenvectors,
        f32(NCHIP, EROWS, 128),
        whole(NCHIP, EROWS, 128),
        [ANY, whole(4, 65536)],
        (mine, eigenvectors),
        size=2 * mega,
    )
    buf, kept = direct(
        inner_products,
        (f32(NCHIP * STEP, 128), hbm(F32, 2 * NCOL, GROUP, 32, 512)),
        (mine, pieces),
        scratch=[pltpu.VMEM((GROUP, NB, 1024), BF16)] * 2 + [pltpu.SemaphoreType.DMA(())],
        out_specs=(VMEM, HBM),
        flops=4 * 10**9,
        size=6 * mega,
    )
    other = lax.ppermute(kept, "core", SWAP)
    arrived = exchange(buf.reshape(NCHIP, STEP, 128), CHIPS)

    part, spread = run(
        sum_products,
        (hbm(F32, NCHIP, GROWS, 128), f32(NCHIP, EROWS, 128)),
        (HBM, whole(NCHIP, EROWS, 128)),
        [whole(NCHIP, STEP, 128)],
        (arrived,),
        scratch=[pltpu.VMEM((GROWS, 128), F32), pltpu.SemaphoreType.DMA((NCHIP,))],
        size=5 * mega,
    )

    block = pl.BlockSpec((2 * NCOL, 1, 32, 512), lambda n, core: (0, lax.rem(n, GROUP), 0, 0))
    early = pl.BlockSpec((1, NB, 1024), lambda n, core: (jnp.minimum(n, GROUP - 1), 0, 0))
    late = pl.BlockSpec((1, NB, 1024), lambda n, core: (jnp.maximum(n - GROUP, 0), 0, 0))
    column = pl.BlockSpec((1024, NB), lambda n, core: (0, jnp.maximum(n - GROUP, 0)))
    split_vectors = hbm(BF16, GROUP, NB, 1024)
    high_b, low_b, high_a, low_a, start, buf, first, cross_high, cross_low = run(
        local_products,
        (
            split_vectors, split_vectors, split_vectors, split_vectors, hbm(F32, 256, 1024),
            hbm(F32, NCHIP * PROWS, 128), hbm(F32, 256, 1024), hbm(BF16, 1024, 1024), hbm(BF16, 1024, 1024),
        ),
        (
            early, early, late, late, whole(256, 1024), whole(NCHIP * PROWS, 128),
            pl.BlockSpec((256, NB), lambda n, core: (0, jnp.maximum(n - GROUP, 0))), column, column,
        ),
        [block, block, whole(NCHIP * EROWS, 128)],
        (kept, other, spread.reshape(NCHIP * EROWS, 128)),
        pin=(0, 1),
        grid=(8,),
        scratch=rows_pair + [pltpu.VMEM((1024, 1024), BF16)] * 2,
        core=core,
        flops=10**10,
        size=24 * mega,
    )
    gram = after(buf, exchange(part, CHIPS)).reshape(ALLROWS, 128)

    count = len(PAIRS)
    factors, own_high, own_low = run(
        invert,
        (hbm(F32, count, NB, NB), bf16(count, NB, NB), bf16(count, NB, NB)),
        (whole(count, NB, NB),) * 3,
        [whole(ALLROWS, 128)],
        (gram,),
    )
    arrived = after(factors, exchange(after(gram, buf, (1,)).reshape(NCHIP, PROWS, 128), CHIPS))
    rows = f32(PROWS, 128)
    projection = run(sum_projection, rows, whole(PROWS, 128), [whole(NCHIP, PROWS, 128)], (arrived,), size=mega)
    found, found_sib = direct(
        solve_both,
        (rows, rows),
        (projection, lax.ppermute(projection, "core", SWAP), own_high, own_low),
        flops=10**8,
        size=3 * mega,
    )
    found = run(
        spread_found,
        f32(NCHIP, PROWS, 128),
        whole(NCHIP, PROWS, 128),
        [whole(PROWS, 128), whole(PROWS, 128)],
        (found, lax.ppermute(found_sib, "core", SWAP)),
        core=core,
        size=mega,
    )
    coefficients = exchange(found, CHIPS)
    factors = after(coefficients, factors, (1,))
    coefficients = coefficients.reshape(NCHIP * PROWS, 128)
    square = pl.BlockSpec((2, NB, NB), lambda n, core: (n, 0, 0))
    first_high, first_low = run(
        pick_factors,
        (bf16(count, NB, NB),) * 2,
        (square,) * 2,
        [square, square],
        (factors, lax.ppermute(factors, "core", SWAP)),
        grid=(count // 2,),
        core=core,
        size=8 * mega,
    )
    buf = direct(
        correct_projection,
        f32(NCHIP * PROWS, 128),
        (coefficients, cross_high, cross_low, first),
        scratch=rows_pair,
        flops=2 * 10**9,
        size=7 * mega,
    )
    middle = direct(
        update,
        f32(256, 1024),
        (coefficients, high_b, low_b, start),
        scratch=rows_pair,
        flops=2 * 10**9,
        size=7 * mega,
    )
    arrived = after(middle, after(first_high, exchange(buf.reshape(NCHIP, PROWS, 128), CHIPS), ()), ())
    found = direct(
        solve_own,
        f32(NCHIP, PROWS, 128),
        (arrived, first_high, first_low),
        scratch=[pltpu.VMEM((PROWS, 128), F32)],
        flops=10**8,
        size=5 * mega,
    )
    coefficients = exchange(found, CHIPS).reshape(NCHIP * PROWS, 128)
    finished = direct(
        update_last,
        f32(2 * NCOL, 32, 512),
        (coefficients, high_a, low_a, middle),
        scratch=rows_pair,
        flops=2 * 10**9,
        size=7 * mega,
    )
    return run(
        place_rows,
        f32(64, 4096),
        whole(64, 4096),
        [whole(2 * NCOL, 32, 512)],
        (exchange(finished, CORE_COLS),),
        scratch=[pltpu.VMEM((2048, 128), F32)],
        size=2 * mega,
    )


def solution(mesh):
    fine = Mesh(mesh.devices.reshape(SIZES), AXES)
    in_specs = (P(AXES, None), P(None, COLS, ("y", "xl", "core")))
    out_specs = P(COLS, ("y", "xl", "core"))
    return jax.shard_map(on_device, mesh=fine, in_specs=in_specs, out_specs=out_specs, check_vma=False)
```

```python
import jax
import jax.numpy as jnp
from jax import lax
from jax.experimental import pallas as pl
from jax.experimental.pallas import tpu as pltpu
from jax.sharding import Mesh, PartitionSpec as P

AXES = ("y", "xl", "core", "z", "xh")
SIZES = (4, 2, 2, 4, 2)
CHIPS = ("y", "xl", "z", "xh")
COLS = ("z", "xh")
CORE_COLS = ("core", "z", "xh")
SWAP = ((0, 1), (1, 0))

NCHIP = 64
NCOL = 8
NB = 256
GROUP = 4
PAIRS = [(i, j) for j in range(GROUP) for i in range(j + 1)]


def place_pieces():
    at, pieces = 0, {}
    for i, j in PAIRS:
        for half in range(2):
            rows = NB // 2 if i == j and half == 0 else NB
            pieces[i, j, half] = (at, rows)
            at += rows
    return at, pieces


ALLROWS, PIECES = place_pieces()
GROWS = ALLROWS // NCHIP
EROWS = 32
STEP = GROWS + EROWS
PROWS = 32
ANY = pl.BlockSpec(memory_space=pl.ANY)
HBM = pl.BlockSpec(memory_space=pltpu.HBM)
VMEM = pl.BlockSpec(memory_space=pltpu.VMEM)
F32 = jnp.float32
BF16 = jnp.bfloat16
NT = (((1,), (1,)), ((), ()))
NN = (((1,), (0,)), ((), ()))


def bf16(*shape):
    return jax.ShapeDtypeStruct(shape, BF16)


def f32(*shape):
    return jax.ShapeDtypeStruct(shape, F32)


def hbm(dtype, *shape):
    return pltpu.HBM(shape, dtype)


def split(value):
    high = value.astype(BF16)
    return high, (value - high.astype(F32)).astype(BF16)


def dot3(a, b, dims):
    def one(x, y):
        return lax.dot_general(x, y, dims, preferred_element_type=F32)

    return one(a[0], b[0]) + (one(a[0], b[1]) + one(a[1], b[0]))


def cut_eigenvectors(after_ref, e_ref, out_ref):
    for core in range(2):
        for c in range(NCOL):
            for t in range(4):
                for k in range(8):
                    at = (((k * 2 + core) * NCOL + c) * 4 + t) * 128
                    out_ref[k * NCOL + c, core * 16 + t * 4 : core * 16 + t * 4 + 4, :] = e_ref[:, at : at + 128]


def cut_vectors(w_ref, out_ref, done):
    copies = []
    for core in range(2):
        for c in range(NCOL):
            to = core * NCOL + c
            first = (1 - core) * GROUP
            copies.append(
                pltpu.make_async_copy(
                    w_ref.at[first : first + GROUP, :, c * 512 : c * 512 + 512], out_ref.at[to], done.at[to]
                )
            )
    for copy in copies:
        copy.start()
    for copy in copies:
        copy.wait()


def whole_block(value):
    return jnp.concatenate([value[:NCOL].reshape(NB, 512), value[NCOL:].reshape(NB, 512)], axis=1)


def inner_products(w_ref, e_ref, out_ref, kept_ref, high_ref, low_ref, buf_ref, done):
    keep = pltpu.make_async_copy(w_ref, kept_ref, done.at[0])
    keep.start()
    for q in range(NCHIP):
        buf_ref[q * STEP + GROWS : q * STEP + STEP, :] = e_ref[q]
    first = PIECES[0, GROUP - 1, 0][0] // GROWS * STEP
    parts = (slice(0, first), slice(first, NCHIP * STEP))
    sends = [
        pltpu.make_async_copy(buf_ref.at[part], out_ref.at[part], done.at[1 + at]) for at, part in enumerate(parts)
    ]
    for j in range(GROUP):
        high_ref[j], low_ref[j] = split(whole_block(w_ref[:, j]))
        if j == GROUP - 1:
            sends[0].start()
        for i in range(j + 1):
            value = dot3((high_ref[i], low_ref[i]), (high_ref[j], low_ref[j]), NT)
            for half in range(2):
                at, rows = PIECES[i, j, half]
                done = 0
                while done < rows:
                    chip, offset = divmod(at + done, GROWS)
                    take = min(rows - done, GROWS - offset)
                    start = chip * STEP + offset
                    buf_ref[start : start + take, :] = value[done : done + take, half * 128 : half * 128 + 128]
                    done += take
    sends[1].start()
    for copy in (keep, *sends):
        copy.wait()


def gather_rows(ref, step, first, high_ref, low_ref, value_ref=None, columns=8):
    for t in range(columns):
        for i in range(4):
            value = ref[pl.ds(first + t * 4 + i, NCHIP, stride=step), :]
            high, low = split(value)
            high_ref[i * 64 : i * 64 + 64, t * 128 : t * 128 + 128] = high
            low_ref[i * 64 : i * 64 + 64, t * 128 : t * 128 + 128] = low
            if value_ref is not None:
                value_ref[i * 64 : i * 64 + 64, t * 128 : t * 128 + 128] = value


def scatter_rows(value, block, buf_ref):
    for half in range(2):
        for i in range(4):
            start = (block * 2 + half) * 4 + i
            buf_ref[pl.ds(start, NCHIP, stride=PROWS), :] = value[
                i * 64 : i * 64 + 64, half * 128 : half * 128 + 128
            ]


def local_products(
    core_ref, mine_ref, other_ref, e_ref,
    high_b_ref, low_b_ref, high_a_ref, low_a_ref, x_ref, buf_ref, first_ref, ch_ref, cl_ref,
    eh_ref, el_ref, bh_ref, bl_ref,
):
    core, n = core_ref[0], pl.program_id(0)

    @pl.when(n == 0)
    def _():
        for part in range(2):
            at = pl.ds(part * 512, 512)
            gather_rows(
                e_ref, EROWS, part * 16, eh_ref.at[:, at], el_ref.at[:, at], x_ref.at[:, at], columns=4
            )

    held = (core == 0) == (n < GROUP)
    high, low = split(jnp.where(held, whole_block(mine_ref[:, 0]), whole_block(other_ref[:, 0])))
    value = dot3((eh_ref[...], el_ref[...]), (high, low), NT)

    @pl.when(n < GROUP)
    def _():
        high_b_ref[0], low_b_ref[0] = high, low
        bh_ref[pl.ds(n * NB, NB), :] = high
        bl_ref[pl.ds(n * NB, NB), :] = low
        scatter_rows(value, n, buf_ref)

    @pl.when(n >= GROUP)
    def _():
        high_a_ref[0], low_a_ref[0] = high, low
        first_ref[...] = value
        for j in range(GROUP):
            rows = slice(j * NB, j * NB + NB)
            ch_ref[rows, :], cl_ref[rows, :] = split(
                dot3((bh_ref[rows, :], bl_ref[rows, :]), (high, low), NT)
            )


def sum_chips(buf_ref, rows):
    def add(q, total):
        return total + buf_ref[q, :rows, :]

    return lax.fori_loop(0, NCHIP, add, jnp.zeros((rows, 128), F32), unroll=8)


def sum_projection(buf_ref, out_ref):
    out_ref[...] = sum_chips(buf_ref, PROWS)


def spread_rows(part, out_ref):
    def spread(q, carry):
        out_ref[q] = part
        return carry

    lax.fori_loop(0, NCHIP, spread, 0, unroll=8)


def sum_products(buf_ref, out_ref, e_ref, part_ref, done):
    copies = [pltpu.make_async_copy(buf_ref.at[:, GROWS:, :], e_ref, done.at[NCHIP])]
    copies[0].start()
    part_ref[...] = sum_chips(buf_ref, GROWS)
    for q in range(NCHIP):
        copies.append(pltpu.make_async_copy(part_ref, out_ref.at[q], done.at[q]))
        copies[-1].start()
    for copy in copies:
        copy.wait()


def spread_found(core_ref, own_ref, sib_ref, high_ref, low_ref, first_ref, out_ref):
    spread_rows(jnp.where(core_ref[0] == 0, own_ref[...], sib_ref[...]), out_ref)


def block_of(g_ref, i, j):
    halves = []
    for half in range(2):
        at, rows = PIECES[i, j, half]
        value = g_ref[at : at + rows, :]
        if rows < NB:
            value = jnp.concatenate([value, jnp.zeros((NB - rows, 128), F32)], axis=0)
        halves.append(value)
    return jnp.concatenate(halves, axis=1)


def invert(g_ref, out_ref, high_ref, low_ref):
    row = lax.broadcasted_iota(jnp.int32, (NB, NB), 0)
    col = lax.broadcasted_iota(jnp.int32, (NB, NB), 1)
    apart = row ^ col
    for index, (i, j) in enumerate(PAIRS):
        value = block_of(g_ref, i, j)
        if i == j:
            diagonal = jnp.where(row == col, 0.5 * value, 0.0)
            down = 1.0 / jnp.sum(diagonal, axis=1, keepdims=True)
            across = 1.0 / jnp.sum(diagonal, axis=0, keepdims=True)
            beside = jnp.where((apart == 1) & (row < col), value, 0.0)
            value = jnp.where(row == col, down, 0.0) - down * beside * across
        out_ref[index] = value
    size = 2
    while size < NB:
        for i in range(GROUP):
            index = PAIRS.index((i, i))
            beside = jnp.where((apart >= size) & (apart < 2 * size) & (row < col), block_of(g_ref, i, i), 0.0)
            value = out_ref[index]
            halves = split(value)
            product = dot3(split(dot3(halves, split(beside), NN)), halves, NN)
            out_ref[index] = value - product
        size *= 2
    for index in range(len(PAIRS)):
        high_ref[index], low_ref[index] = split(out_ref[index])


def pick_factors(core_ref, own_ref, sib_ref, high_ref, low_ref):
    high_ref[...], low_ref[...] = split(jnp.where(core_ref[0] == 1, own_ref[...], sib_ref[...]))


def solve(rows_of, high_ref, low_ref, keep):
    def factor(i, j):
        index = PAIRS.index((i, j))
        return high_ref[index], low_ref[index]

    found = {}
    for b in range(GROUP - 1, -1, -1):
        rest = jnp.concatenate([rows_of(b * 2), rows_of(b * 2 + 1)], axis=1)
        for later in range(GROUP - 1, b, -1):
            rest = rest - dot3(found[later], factor(b, later), NT)
        value = dot3(split(rest), factor(b, b), NT)
        found[b] = split(value)
        for half in range(2):
            keep(b * 2 + half, value[:, half * 128 : half * 128 + 128])


def solve_both(own_ref, sib_ref, high_ref, low_ref, c_own_ref, c_sib_ref):
    def rows_of(t):
        return jnp.concatenate([own_ref[t * 4 : t * 4 + 4, :], sib_ref[t * 4 : t * 4 + 4, :]], axis=0)

    def keep(t, value):
        c_own_ref[t * 4 : t * 4 + 4, :] = value[0:4]
        c_sib_ref[t * 4 : t * 4 + 4, :] = value[4:8]

    solve(rows_of, high_ref, low_ref, keep)


def solve_own(buf_ref, high_ref, low_ref, out_ref, c_ref):
    c_ref[...] = sum_chips(buf_ref, PROWS)

    def rows_of(t):
        return jnp.concatenate([c_ref[t * 4 : t * 4 + 4, :]] * 2, axis=0)

    def keep(t, value):
        c_ref[t * 4 : t * 4 + 4, :] = value[0:4]

    solve(rows_of, high_ref, low_ref, keep)
    spread_rows(c_ref[...], out_ref)


def correct_projection(c_ref, gh_ref, gl_ref, first_ref, buf_ref, ch_ref, cl_ref):
    gather_rows(c_ref, PROWS, 0, ch_ref, cl_ref)
    for n in range(GROUP):
        at = slice(n * NB, n * NB + NB)
        value = first_ref[:, at] - dot3((ch_ref[...], cl_ref[...]), (gh_ref[:, at], gl_ref[:, at]), NN)
        scatter_rows(value, n, buf_ref)


def updated(n, high_ref, low_ref, x_ref, ch_ref, cl_ref):
    at = slice(n * NB, n * NB + NB)
    vectors = (high_ref[:, :, at].reshape(1024, NB), low_ref[:, :, at].reshape(1024, NB))
    return x_ref[:, at] - dot3((ch_ref[...], cl_ref[...]), vectors, NN)


def update(c_ref, high_ref, low_ref, x_ref, out_ref, ch_ref, cl_ref):
    gather_rows(c_ref, PROWS, 0, ch_ref, cl_ref)
    for n in range(4):
        out_ref[:, n * NB : n * NB + NB] = updated(n, high_ref, low_ref, x_ref, ch_ref, cl_ref)


def update_last(c_ref, high_ref, low_ref, x_ref, out_ref, ch_ref, cl_ref):
    gather_rows(c_ref, PROWS, 0, ch_ref, cl_ref)
    for n in range(4):
        value = updated(n, high_ref, low_ref, x_ref, ch_ref, cl_ref)
        at = n % 2 * NB
        for c in range(NCOL):
            for i in range(4):
                rows = slice(i * 64 + c * 8, i * 64 + c * 8 + 8)
                out_ref[n // 2 * NCOL + c, i * 8 : i * 8 + 8, at : at + NB] = value[rows, :]


def pass_on(after_ref, in_ref, out_ref):
    pass


def place_rows(in_ref, out_ref, held_ref):
    for c in range(NCOL):
        for t in range(4):
            at = c * 512 + t * 128
            for core in range(2):
                for i in range(4):
                    held_ref[pl.ds((c * 4 + t) * 64 + core * 32 + i, 8, stride=4), :] = in_ref[
                        core * NCOL + c, i * 8 : i * 8 + 8, t * 128 : t * 128 + 128
                    ]
            out_ref[:, at : at + 128] = held_ref[(c * 4 + t) * 64 : (c * 4 + t) * 64 + 64, :]


def whole(*shape):
    return pl.BlockSpec(shape, lambda *_: (0,) * len(shape))


def run(kernel, out_shape, out_specs, in_specs, operands, grid=(1,), scratch=(), core=None, flops=0, size=0, limit=32, pin=(), **options):
    operands = [in_hbm(value) if at in pin else value for at, value in enumerate(operands)]
    spec = pltpu.PrefetchScalarGridSpec(
        num_scalar_prefetch=0 if core is None else 1,
        grid=grid,
        in_specs=in_specs,
        out_specs=out_specs,
        scratch_shapes=list(scratch),
    )
    built = pl.pallas_call(
        kernel,
        out_shape=out_shape,
        grid_spec=spec,
        compiler_params=pltpu.CompilerParams(vmem_limit_bytes=limit * 2**20),
        cost_estimate=pl.CostEstimate(flops=flops, bytes_accessed=size, transcendentals=0),
        **options,
    )
    return built(*operands) if core is None else built(core, *operands)


def direct(kernel, out_shape, operands, scratch=(), out_specs=None, flops=0, size=0, limit=32):
    return pl.pallas_call(
        kernel,
        out_shape=out_shape,
        in_specs=[VMEM] * len(operands),
        out_specs=jax.tree.map(lambda _: VMEM, out_shape) if out_specs is None else out_specs,
        scratch_shapes=list(scratch),
        compiler_params=pltpu.CompilerParams(vmem_limit_bytes=limit * 2**20),
        cost_estimate=pl.CostEstimate(flops=flops, bytes_accessed=size, transcendentals=0),
    )(*operands)


def in_hbm(value):
    return pltpu.with_memory_space_constraint(value, pltpu.HBM)


def in_vmem(value):
    return pltpu.with_memory_space_constraint(value, pltpu.VMEM)


def exchange(value, axes):
    return lax.all_to_all(value, axes, 0, 0, tiled=True)


def on_device(eigenvectors, reflectors):
    core = lax.axis_index("core").astype(jnp.int32).reshape(1)
    mega = 2**20
    rows_pair = [pltpu.VMEM((256, 1024), BF16)] * 2

    def after(earlier, value, pin=(0,)):
        return run(
            pass_on, jax.ShapeDtypeStruct(value.shape, F32), ANY, [ANY, ANY], (earlier, value), pin=pin, size=1024, input_output_aliases={1: 0}
        )

    vectors = run(
        cut_vectors,
        f32(2 * NCOL, GROUP, 32, 512),
        whole(2 * NCOL, GROUP, 32, 512),
        [HBM],
        (reflectors,),
        pin=(0,),
        scratch=[pltpu.SemaphoreType.DMA((2 * NCOL,))],
        size=8 * mega,
    )
    mine = exchange(vectors, CORE_COLS)
    pieces = run(
        cut_eigenvectors,
        f32(NCHIP, EROWS, 128),
        whole(NCHIP, EROWS, 128),
        [ANY, whole(4, 65536)],
        (mine, eigenvectors),
        size=2 * mega,
    )
    buf, kept = direct(
        inner_products,
        (hbm(F32, NCHIP * STEP, 128), hbm(F32, 2 * NCOL, GROUP, 32, 512)),
        (mine, pieces),
        scratch=[pltpu.VMEM((GROUP, NB, 1024), BF16)] * 2
        + [pltpu.VMEM((NCHIP * STEP, 128), F32), pltpu.SemaphoreType.DMA((3,))],
        out_specs=(HBM, HBM),
        flops=4 * 10**9,
        size=6 * mega,
    )
    other = lax.ppermute(kept, "core", SWAP)
    arrived = exchange(buf.reshape(NCHIP, STEP, 128), CHIPS)

    part, spread = run(
        sum_products,
        (hbm(F32, NCHIP, GROWS, 128), hbm(F32, NCHIP, EROWS, 128)),
        (HBM, HBM),
        [whole(NCHIP, STEP, 128)],
        (arrived,),
        scratch=[pltpu.VMEM((GROWS, 128), F32), pltpu.SemaphoreType.DMA((NCHIP + 1,))],
        size=5 * mega,
    )

    block = pl.BlockSpec((2 * NCOL, 1, 32, 512), lambda n, core: (0, lax.rem(n, GROUP), 0, 0))
    early = pl.BlockSpec((1, NB, 1024), lambda n, core: (jnp.minimum(n, GROUP - 1), 0, 0))
    late = pl.BlockSpec((1, NB, 1024), lambda n, core: (jnp.maximum(n - GROUP, 0), 0, 0))
    column = pl.BlockSpec((1024, NB), lambda n, core: (0, jnp.maximum(n - GROUP, 0)))
    split_vectors = hbm(BF16, GROUP, NB, 1024)
    high_b, low_b, high_a, low_a, start, buf, first, cross_high, cross_low = run(
        local_products,
        (
            split_vectors, split_vectors, split_vectors, split_vectors, hbm(F32, 256, 1024),
            hbm(F32, NCHIP * PROWS, 128), hbm(F32, 256, 1024), hbm(BF16, 1024, 1024), hbm(BF16, 1024, 1024),
        ),
        (
            early, early, late, late, whole(256, 1024), whole(NCHIP * PROWS, 128),
            pl.BlockSpec((256, NB), lambda n, core: (0, jnp.maximum(n - GROUP, 0))), column, column,
        ),
        [block, block, whole(NCHIP * EROWS, 128)],
        (kept, other, spread.reshape(NCHIP * EROWS, 128)),
        pin=(0, 1),
        grid=(8,),
        scratch=rows_pair + [pltpu.VMEM((1024, 1024), BF16)] * 2,
        core=core,
        flops=10**10,
        size=24 * mega,
    )
    gram = after(buf, exchange(part, CHIPS)).reshape(ALLROWS, 128)

    count = len(PAIRS)
    factors, own_high, own_low = run(
        invert,
        (hbm(F32, count, NB, NB), bf16(count, NB, NB), bf16(count, NB, NB)),
        (whole(count, NB, NB),) * 3,
        [whole(ALLROWS, 128)],
        (gram,),
    )
    arrived = after(factors, exchange(after(gram, buf, (1,)).reshape(NCHIP, PROWS, 128), CHIPS))
    rows = f32(PROWS, 128)
    projection = run(sum_projection, rows, whole(PROWS, 128), [whole(NCHIP, PROWS, 128)], (arrived,), size=mega)
    found, found_sib = direct(
        solve_both,
        (rows, rows),
        (projection, lax.ppermute(projection, "core", SWAP), own_high, own_low),
        flops=10**8,
        size=3 * mega,
    )
    found = run(
        spread_found,
        f32(NCHIP, PROWS, 128),
        whole(NCHIP, PROWS, 128),
        [whole(PROWS, 128), whole(PROWS, 128), ANY, ANY, ANY],
        (found, lax.ppermute(found_sib, "core", SWAP), in_vmem(cross_high), in_vmem(cross_low), in_vmem(first)),
        core=core,
        size=mega,
    )
    coefficients = exchange(found, CHIPS)
    factors = after(coefficients, factors, (1,))
    coefficients = coefficients.reshape(NCHIP * PROWS, 128)
    square = pl.BlockSpec((2, NB, NB), lambda n, core: (n, 0, 0))
    first_high, first_low = run(
        pick_factors,
        (bf16(count, NB, NB),) * 2,
        (square,) * 2,
        [square, square],
        (factors, lax.ppermute(factors, "core", SWAP)),
        grid=(count // 2,),
        core=core,
        size=8 * mega,
    )
    buf = direct(
        correct_projection,
        f32(NCHIP * PROWS, 128),
        (coefficients, cross_high, cross_low, first),
        scratch=rows_pair,
        flops=2 * 10**9,
        size=7 * mega,
    )
    middle = direct(
        update,
        f32(256, 1024),
        (coefficients, high_b, low_b, start),
        scratch=rows_pair,
        flops=2 * 10**9,
        size=7 * mega,
    )
    arrived = after(middle, after(in_vmem(first_high), exchange(buf.reshape(NCHIP, PROWS, 128), CHIPS), ()), ())
    found = direct(
        solve_own,
        f32(NCHIP, PROWS, 128),
        (arrived, first_high, first_low),
        scratch=[pltpu.VMEM((PROWS, 128), F32)],
        flops=10**8,
        size=5 * mega,
    )
    coefficients = exchange(found, CHIPS).reshape(NCHIP * PROWS, 128)
    finished = direct(
        update_last,
        f32(2 * NCOL, 32, 512),
        (coefficients, high_a, low_a, middle),
        scratch=rows_pair,
        flops=2 * 10**9,
        size=7 * mega,
    )
    return run(
        place_rows,
        f32(64, 4096),
        whole(64, 4096),
        [whole(2 * NCOL, 32, 512)],
        (exchange(finished, CORE_COLS),),
        scratch=[pltpu.VMEM((2048, 128), F32)],
        size=2 * mega,
    )


def solution(mesh):
    fine = Mesh(mesh.devices.reshape(SIZES), AXES)
    in_specs = (P(AXES, None), P(None, COLS, ("y", "xl", "core")))
    out_specs = P(COLS, ("y", "xl", "core"))
    return jax.shard_map(on_device, mesh=fine, in_specs=in_specs, out_specs=out_specs, check_vma=False)
```

```python
import functools

import jax
import jax.numpy as jnp
from jax import lax
from jax.experimental import pallas as pl
from jax.experimental.pallas import tpu as pltpu
from jax.sharding import Mesh, PartitionSpec as P

AXES = ("y", "xl", "core", "z", "xh")
SIZES = (4, 2, 2, 4, 2)
CHIPS = ("y", "xl", "z", "xh")
COLS = ("z", "xh")
CORE_COLS = ("core", "z", "xh")
SWAP = ((0, 1), (1, 0))

NCHIP = 64
NCOL = 8
NB = 256
GROUP = 4
PAIRS = [(i, j) for j in range(GROUP) for i in range(j + 1)]
USES = [(i, j) for i in range(GROUP - 1, -1, -1) for j in range(GROUP - 1, i - 1, -1)]


def place_pieces():
    at, pieces = 0, {}
    for i, j in PAIRS:
        for half in range(2):
            rows = NB // 2 if i == j and half == 0 else NB
            pieces[i, j, half] = (at, rows)
            at += rows
    return at, pieces


ALLROWS, PIECES = place_pieces()
GROWS = ALLROWS // NCHIP
EROWS = 32
STEP = GROWS + EROWS
PROWS = 32
ANY = pl.BlockSpec(memory_space=pl.ANY)
HBM = pl.BlockSpec(memory_space=pltpu.HBM)
VMEM = pl.BlockSpec(memory_space=pltpu.VMEM)
F32 = jnp.float32
BF16 = jnp.bfloat16
NT = (((1,), (1,)), ((), ()))
NN = (((1,), (0,)), ((), ()))


def bf16(*shape):
    return jax.ShapeDtypeStruct(shape, BF16)


def f32(*shape):
    return jax.ShapeDtypeStruct(shape, F32)


def hbm(dtype, *shape):
    return pltpu.HBM(shape, dtype)


def split(value):
    high = value.astype(BF16)
    return high, (value - high.astype(F32)).astype(BF16)


def dot3(a, b, dims):
    def one(x, y):
        return lax.dot_general(x, y, dims, preferred_element_type=F32)

    return one(a[0], b[0]) + (one(a[0], b[1]) + one(a[1], b[0]))


def cut_eigenvectors(after_ref, e_ref, out_ref):
    for core in range(2):
        for c in range(NCOL):
            for t in range(4):
                for k in range(8):
                    at = (((k * 2 + core) * NCOL + c) * 4 + t) * 128
                    out_ref[k * NCOL + c, core * 16 + t * 4 : core * 16 + t * 4 + 4, :] = e_ref[:, at : at + 128]


def cut_vectors(w_ref, out_ref, done):
    copies = []
    for core in range(2):
        for c in range(NCOL):
            to = core * NCOL + c
            first = (1 - core) * GROUP
            copies.append(
                pltpu.make_async_copy(
                    w_ref.at[first : first + GROUP, :, c * 512 : c * 512 + 512], out_ref.at[to], done.at[to]
                )
            )
    for copy in copies:
        copy.start()
    for copy in copies:
        copy.wait()


def whole_block(value):
    return jnp.concatenate([value[:NCOL].reshape(NB, 512), value[NCOL:].reshape(NB, 512)], axis=1)


def inner_products(w_ref, e_ref, out_ref, kept_ref, high_ref, low_ref, buf_ref, done):
    keep = pltpu.make_async_copy(w_ref, kept_ref, done.at[0])
    keep.start()
    for q in range(NCHIP):
        buf_ref[q * STEP + GROWS : q * STEP + STEP, :] = e_ref[q]
    first = PIECES[0, GROUP - 1, 0][0] // GROWS * STEP
    parts = (slice(0, first), slice(first, NCHIP * STEP))
    sends = [
        pltpu.make_async_copy(buf_ref.at[part], out_ref.at[part], done.at[1 + at]) for at, part in enumerate(parts)
    ]
    for j in range(GROUP):
        high_ref[j], low_ref[j] = split(whole_block(w_ref[:, j]))
        if j == GROUP - 1:
            sends[0].start()
        for i in range(j + 1):
            value = dot3((high_ref[i], low_ref[i]), (high_ref[j], low_ref[j]), NT)
            for half in range(2):
                at, rows = PIECES[i, j, half]
                done = 0
                while done < rows:
                    chip, offset = divmod(at + done, GROWS)
                    take = min(rows - done, GROWS - offset)
                    start = chip * STEP + offset
                    buf_ref[start : start + take, :] = value[done : done + take, half * 128 : half * 128 + 128]
                    done += take
    sends[1].start()
    for copy in (keep, *sends):
        copy.wait()


def gather_rows(ref, step, first, high_ref, low_ref, value_ref=None, columns=8):
    for t in range(columns):
        for i in range(4):
            value = ref[pl.ds(first + t * 4 + i, NCHIP, stride=step), :]
            high, low = split(value)
            high_ref[i * 64 : i * 64 + 64, t * 128 : t * 128 + 128] = high
            low_ref[i * 64 : i * 64 + 64, t * 128 : t * 128 + 128] = low
            if value_ref is not None:
                value_ref[i * 64 : i * 64 + 64, t * 128 : t * 128 + 128] = value


def scatter_rows(value, block, buf_ref):
    for half in range(2):
        for i in range(4):
            start = (block * 2 + half) * 4 + i
            buf_ref[pl.ds(start, NCHIP, stride=PROWS), :] = value[
                i * 64 : i * 64 + 64, half * 128 : half * 128 + 128
            ]


def local_products(
    core_ref, mine_ref, other_ref, e_ref,
    high_b_ref, low_b_ref, high_a_ref, low_a_ref, x_ref, buf_ref, first_ref, ch_ref, cl_ref,
    eh_ref, el_ref, bh_ref, bl_ref,
):
    core, n = core_ref[0], pl.program_id(0)

    @pl.when(n == 0)
    def _():
        for part in range(2):
            at = pl.ds(part * 512, 512)
            gather_rows(
                e_ref, EROWS, part * 16, eh_ref.at[:, at], el_ref.at[:, at], x_ref.at[:, at], columns=4
            )

    held = (core == 0) == (n < GROUP)
    high, low = split(jnp.where(held, whole_block(mine_ref[:, 0]), whole_block(other_ref[:, 0])))
    value = dot3((eh_ref[...], el_ref[...]), (high, low), NT)

    @pl.when(n < GROUP)
    def _():
        high_b_ref[0], low_b_ref[0] = high, low
        bh_ref[pl.ds(n * NB, NB), :] = high
        bl_ref[pl.ds(n * NB, NB), :] = low
        scatter_rows(value, n, buf_ref)

    @pl.when(n >= GROUP)
    def _():
        high_a_ref[0], low_a_ref[0] = high, low
        first_ref[...] = value
        for j in range(GROUP):
            rows = slice(j * NB, j * NB + NB)
            ch_ref[rows, :], cl_ref[rows, :] = split(
                dot3((bh_ref[rows, :], bl_ref[rows, :]), (high, low), NT)
            )


def sum_chips(buf_ref, rows):
    def add(q, total):
        return total + buf_ref[q, :rows, :]

    return lax.fori_loop(0, NCHIP, add, jnp.zeros((rows, 128), F32), unroll=8)


def spread_rows(part, out_ref):
    def spread(q, carry):
        out_ref[q] = part
        return carry

    lax.fori_loop(0, NCHIP, spread, 0, unroll=8)


def sum_products(buf_ref, out_ref, e_ref, part_ref, done):
    copies = [pltpu.make_async_copy(buf_ref.at[:, GROWS:, :], e_ref, done.at[NCHIP])]
    copies[0].start()
    part_ref[...] = sum_chips(buf_ref, GROWS)
    for q in range(NCHIP):
        copies.append(pltpu.make_async_copy(part_ref, out_ref.at[q], done.at[q]))
        copies[-1].start()
    for copy in copies:
        copy.wait()


def block_of(g_ref, i, j):
    halves = []
    for half in range(2):
        at, rows = PIECES[i, j, half]
        value = g_ref[at : at + rows, :]
        if rows < NB:
            value = jnp.concatenate([value, jnp.zeros((NB - rows, 128), F32)], axis=0)
        halves.append(value)
    return jnp.concatenate(halves, axis=1)


def invert(holder, core_ref, own_ref, sib_ref, *refs):
    high_ref, low_ref, g_ref, held_ref = refs[-4:]
    g_ref[...] = jnp.where(core_ref[0] == holder, own_ref[...], sib_ref[...])
    row = lax.broadcasted_iota(jnp.int32, (NB, NB), 0)
    col = lax.broadcasted_iota(jnp.int32, (NB, NB), 1)
    apart = row ^ col
    for index, (i, j) in enumerate(USES):
        value = block_of(g_ref, i, j)
        if i != j:
            high_ref[index], low_ref[index] = split(value)
            continue
        diagonal = jnp.where(row == col, 0.5 * value, 0.0)
        down = 1.0 / jnp.sum(diagonal, axis=1, keepdims=True)
        across = 1.0 / jnp.sum(diagonal, axis=0, keepdims=True)
        beside = jnp.where((apart == 1) & (row < col), value, 0.0)
        held_ref[i] = jnp.where(row == col, down, 0.0) - down * beside * across
    size = 2
    while size < NB:
        for i in range(GROUP):
            beside = jnp.where((apart >= size) & (apart < 2 * size) & (row < col), block_of(g_ref, i, i), 0.0)
            value = held_ref[i]
            halves = split(value)
            product = dot3(split(dot3(halves, split(beside), NN)), halves, NN)
            held_ref[i] = value - product
        size *= 2
    for i in range(GROUP):
        index = USES.index((i, i))
        high_ref[index], low_ref[index] = split(held_ref[i])


def solve(rows_of, factor, keep):
    found = {}
    for b in range(GROUP - 1, -1, -1):
        rest = jnp.concatenate([rows_of(b * 2), rows_of(b * 2 + 1)], axis=1)
        for later in range(GROUP - 1, b, -1):
            rest = rest - dot3(found[later], factor(b, later), NT)
        value = dot3(split(rest), factor(b, b), NT)
        found[b] = split(value)
        for half in range(2):
            keep(b * 2 + half, value[:, half * 128 : half * 128 + 128])


def solve_own(buf_ref, high_from, low_from, out_ref, high_ref, low_ref, c_ref, done):
    parts = (slice(0, 3), slice(3, len(USES)))
    fetches = []
    for at, part in enumerate(parts):
        fetches.append(pltpu.make_async_copy(high_from.at[part], high_ref.at[part], done.at[0, at]))
        fetches.append(pltpu.make_async_copy(low_from.at[part], low_ref.at[part], done.at[1, at]))
    for fetch in fetches:
        fetch.start()
    c_ref[...] = sum_chips(buf_ref, PROWS)

    def rows_of(t):
        return jnp.concatenate([c_ref[t * 4 : t * 4 + 4, :]] * 2, axis=0)

    def keep(t, value):
        c_ref[t * 4 : t * 4 + 4, :] = value[0:4]

    def factor(i, j):
        index = USES.index((i, j))
        if index in (0, 3):
            for fetch in fetches[0:2] if index == 0 else fetches[2:4]:
                fetch.wait()
        return high_ref[index], low_ref[index]

    solve(rows_of, factor, keep)
    spread_rows(c_ref[...], out_ref)


def correct_projection(c_ref, gh_ref, gl_ref, first_ref, buf_ref, ch_ref, cl_ref):
    gather_rows(c_ref, PROWS, 0, ch_ref, cl_ref)
    for n in range(GROUP):
        at = slice(n * NB, n * NB + NB)
        value = first_ref[:, at] - dot3((ch_ref[...], cl_ref[...]), (gh_ref[:, at], gl_ref[:, at]), NN)
        scatter_rows(value, n, buf_ref)


def updated(n, high_ref, low_ref, x_ref, ch_ref, cl_ref):
    at = slice(n * NB, n * NB + NB)
    vectors = (high_ref[:, :, at].reshape(1024, NB), low_ref[:, :, at].reshape(1024, NB))
    return x_ref[:, at] - dot3((ch_ref[...], cl_ref[...]), vectors, NN)


def update(c_ref, high_ref, low_ref, x_ref, out_ref, ch_ref, cl_ref):
    gather_rows(c_ref, PROWS, 0, ch_ref, cl_ref)
    for n in range(4):
        out_ref[:, n * NB : n * NB + NB] = updated(n, high_ref, low_ref, x_ref, ch_ref, cl_ref)


def update_last(c_ref, high_ref, low_ref, x_ref, out_ref, ch_ref, cl_ref):
    gather_rows(c_ref, PROWS, 0, ch_ref, cl_ref)
    for n in range(4):
        value = updated(n, high_ref, low_ref, x_ref, ch_ref, cl_ref)
        at = n % 2 * NB
        for c in range(NCOL):
            for i in range(4):
                rows = slice(i * 64 + c * 8, i * 64 + c * 8 + 8)
                out_ref[n // 2 * NCOL + c, i * 8 : i * 8 + 8, at : at + NB] = value[rows, :]


def pass_on(after_ref, in_ref, out_ref):
    pass


def place_rows(in_ref, out_ref, held_ref):
    for c in range(NCOL):
        for t in range(4):
            at = c * 512 + t * 128
            for core in range(2):
                for i in range(4):
                    held_ref[pl.ds((c * 4 + t) * 64 + core * 32 + i, 8, stride=4), :] = in_ref[
                        core * NCOL + c, i * 8 : i * 8 + 8, t * 128 : t * 128 + 128
                    ]
            out_ref[:, at : at + 128] = held_ref[(c * 4 + t) * 64 : (c * 4 + t) * 64 + 64, :]


def whole(*shape):
    return pl.BlockSpec(shape, lambda *_: (0,) * len(shape))


def run(kernel, out_shape, out_specs, in_specs, operands, grid=(1,), scratch=(), core=None, flops=0, size=0, limit=32, pin=(), **options):
    operands = [in_hbm(value) if at in pin else value for at, value in enumerate(operands)]
    spec = pltpu.PrefetchScalarGridSpec(
        num_scalar_prefetch=0 if core is None else 1,
        grid=grid,
        in_specs=in_specs,
        out_specs=out_specs,
        scratch_shapes=list(scratch),
    )
    built = pl.pallas_call(
        kernel,
        out_shape=out_shape,
        grid_spec=spec,
        compiler_params=pltpu.CompilerParams(vmem_limit_bytes=limit * 2**20),
        cost_estimate=pl.CostEstimate(flops=flops, bytes_accessed=size, transcendentals=0),
        **options,
    )
    return built(*operands) if core is None else built(core, *operands)


def direct(kernel, out_shape, operands, scratch=(), in_specs=None, out_specs=None, flops=0, size=0, limit=32):
    return pl.pallas_call(
        kernel,
        out_shape=out_shape,
        in_specs=[VMEM] * len(operands) if in_specs is None else in_specs,
        out_specs=jax.tree.map(lambda _: VMEM, out_shape) if out_specs is None else out_specs,
        scratch_shapes=list(scratch),
        compiler_params=pltpu.CompilerParams(vmem_limit_bytes=limit * 2**20),
        cost_estimate=pl.CostEstimate(flops=flops, bytes_accessed=size, transcendentals=0),
    )(*operands)


def in_hbm(value):
    return pltpu.with_memory_space_constraint(value, pltpu.HBM)


def in_vmem(value):
    return pltpu.with_memory_space_constraint(value, pltpu.VMEM)


def exchange(value, axes):
    return lax.all_to_all(value, axes, 0, 0, tiled=True)


def on_device(eigenvectors, reflectors):
    core = lax.axis_index("core").astype(jnp.int32).reshape(1)
    mega = 2**20
    rows_pair = [pltpu.VMEM((256, 1024), BF16)] * 2

    def after(earlier, value, pin=(0,)):
        return run(
            pass_on, jax.ShapeDtypeStruct(value.shape, F32), ANY, [ANY, ANY], (earlier, value), pin=pin, size=1024, input_output_aliases={1: 0}
        )

    vectors = run(
        cut_vectors,
        f32(2 * NCOL, GROUP, 32, 512),
        whole(2 * NCOL, GROUP, 32, 512),
        [HBM],
        (reflectors,),
        pin=(0,),
        scratch=[pltpu.SemaphoreType.DMA((2 * NCOL,))],
        size=8 * mega,
    )
    mine = exchange(vectors, CORE_COLS)
    pieces = run(
        cut_eigenvectors,
        f32(NCHIP, EROWS, 128),
        whole(NCHIP, EROWS, 128),
        [ANY, whole(4, 65536)],
        (mine, eigenvectors),
        size=2 * mega,
    )
    buf, kept = direct(
        inner_products,
        (hbm(F32, NCHIP * STEP, 128), hbm(F32, 2 * NCOL, GROUP, 32, 512)),
        (mine, pieces),
        scratch=[pltpu.VMEM((GROUP, NB, 1024), BF16)] * 2
        + [pltpu.VMEM((NCHIP * STEP, 128), F32), pltpu.SemaphoreType.DMA((3,))],
        out_specs=(HBM, HBM),
        flops=4 * 10**9,
        size=6 * mega,
    )
    other = lax.ppermute(kept, "core", SWAP)
    arrived = exchange(buf.reshape(NCHIP, STEP, 128), CHIPS)

    part, spread = run(
        sum_products,
        (hbm(F32, NCHIP, GROWS, 128), hbm(F32, NCHIP, EROWS, 128)),
        (HBM, HBM),
        [whole(NCHIP, STEP, 128)],
        (arrived,),
        scratch=[pltpu.VMEM((GROWS, 128), F32), pltpu.SemaphoreType.DMA((NCHIP + 1,))],
        size=5 * mega,
    )

    block = pl.BlockSpec((2 * NCOL, 1, 32, 512), lambda n, core: (0, lax.rem(n, GROUP), 0, 0))
    early = pl.BlockSpec((1, NB, 1024), lambda n, core: (jnp.minimum(n, GROUP - 1), 0, 0))
    late = pl.BlockSpec((1, NB, 1024), lambda n, core: (jnp.maximum(n - GROUP, 0), 0, 0))
    column = pl.BlockSpec((1024, NB), lambda n, core: (0, jnp.maximum(n - GROUP, 0)))
    split_vectors = hbm(BF16, GROUP, NB, 1024)
    high_b, low_b, high_a, low_a, start, buf, first, cross_high, cross_low = run(
        local_products,
        (
            split_vectors, split_vectors, split_vectors, split_vectors, hbm(F32, 256, 1024),
            hbm(F32, NCHIP * PROWS, 128), hbm(F32, 256, 1024), hbm(BF16, 1024, 1024), hbm(BF16, 1024, 1024),
        ),
        (
            early, early, late, late, whole(256, 1024), whole(NCHIP * PROWS, 128),
            pl.BlockSpec((256, NB), lambda n, core: (0, jnp.maximum(n - GROUP, 0))), column, column,
        ),
        [block, block, whole(NCHIP * EROWS, 128)],
        (kept, other, spread.reshape(NCHIP * EROWS, 128)),
        pin=(0, 1),
        grid=(8,),
        scratch=rows_pair + [pltpu.VMEM((1024, 1024), BF16)] * 2,
        core=core,
        flops=10**10,
        size=24 * mega,
    )
    gram = after(buf, exchange(part, CHIPS)).reshape(ALLROWS, 128)

    count = len(PAIRS)
    gram_sib = lax.ppermute(gram, "core", SWAP)

    def factors_of(holder, later=()):
        return run(
            functools.partial(invert, holder),
            (hbm(BF16, count, NB, NB),) * 2,
            (whole(count, NB, NB),) * 2,
            [whole(ALLROWS, 128)] * 2 + [ANY] * len(later),
            (gram, gram_sib, *later),
            scratch=[pltpu.VMEM((ALLROWS, 128), F32), pltpu.VMEM((GROUP, NB, NB), F32)],
            core=core,
        )

    def coefficients_of(arrived, high, low):
        found = direct(
            solve_own,
            f32(NCHIP, PROWS, 128),
            (arrived, in_hbm(high), in_hbm(low)),
            scratch=[
                pltpu.VMEM((count, NB, NB), BF16),
                pltpu.VMEM((count, NB, NB), BF16),
                pltpu.VMEM((PROWS, 128), F32),
                pltpu.SemaphoreType.DMA((2, 2)),
            ],
            in_specs=[VMEM, HBM, HBM],
            flops=10**8,
            size=5 * mega,
        )
        return exchange(found, CHIPS).reshape(NCHIP * PROWS, 128)

    high, low = factors_of(0, (in_vmem(cross_high), in_vmem(cross_low), in_vmem(first)))
    arrived = after(high, exchange(after(gram, buf, (1,)).reshape(NCHIP, PROWS, 128), CHIPS))
    coefficients = coefficients_of(arrived, high, low)
    buf = direct(
        correct_projection,
        hbm(F32, NCHIP * PROWS, 128),
        (coefficients, cross_high, cross_low, first),
        scratch=rows_pair,
        flops=2 * 10**9,
        size=7 * mega,
    )
    middle = direct(
        update,
        f32(256, 1024),
        (coefficients, high_b, low_b, start),
        scratch=rows_pair,
        flops=2 * 10**9,
        size=7 * mega,
    )
    high, low = factors_of(1)
    arrived = after(middle, after(high, exchange(buf.reshape(NCHIP, PROWS, 128), CHIPS)), ())
    coefficients = coefficients_of(arrived, high, low)
    finished = direct(
        update_last,
        f32(2 * NCOL, 32, 512),
        (coefficients, high_a, low_a, middle),
        scratch=rows_pair,
        flops=2 * 10**9,
        size=7 * mega,
    )
    return run(
        place_rows,
        f32(64, 4096),
        whole(64, 4096),
        [whole(2 * NCOL, 32, 512)],
        (exchange(finished, CORE_COLS),),
        scratch=[pltpu.VMEM((2048, 128), F32)],
        size=2 * mega,
    )


def solution(mesh):
    fine = Mesh(mesh.devices.reshape(SIZES), AXES)
    in_specs = (P(AXES, None), P(None, COLS, ("y", "xl", "core")))
    out_specs = P(COLS, ("y", "xl", "core"))
    return jax.shard_map(on_device, mesh=fine, in_specs=in_specs, out_specs=out_specs, check_vma=False)
```

```python
import functools

import jax
import jax.numpy as jnp
from jax import lax
from jax.experimental import pallas as pl
from jax.experimental.pallas import tpu as pltpu
from jax.sharding import Mesh, PartitionSpec as P

AXES = ("y", "xl", "core", "z", "xh")
SIZES = (4, 2, 2, 4, 2)
CHIPS = ("y", "xl", "z", "xh")
COLS = ("z", "xh")
CORE_COLS = ("core", "z", "xh")
SWAP = ((0, 1), (1, 0))

NCHIP = 64
NCOL = 8
NB = 256
GROUP = 4
PAIRS = [(i, j) for j in range(GROUP) for i in range(j + 1)]
USES = [(i, j) for i in range(GROUP - 1, -1, -1) for j in range(GROUP - 1, i - 1, -1)]


def place_pieces():
    at, pieces = 0, {}
    for i, j in PAIRS:
        for half in range(2):
            rows = NB // 2 if i == j and half == 0 else NB
            pieces[i, j, half] = (at, rows)
            at += rows
    return at, pieces


ALLROWS, PIECES = place_pieces()
GROWS = ALLROWS // NCHIP
EROWS = 32
STEP = GROWS + EROWS
PROWS = 32
ANY = pl.BlockSpec(memory_space=pl.ANY)
HBM = pl.BlockSpec(memory_space=pltpu.HBM)
VMEM = pl.BlockSpec(memory_space=pltpu.VMEM)
F32 = jnp.float32
BF16 = jnp.bfloat16
NT = (((1,), (1,)), ((), ()))
NN = (((1,), (0,)), ((), ()))


def bf16(*shape):
    return jax.ShapeDtypeStruct(shape, BF16)


def f32(*shape):
    return jax.ShapeDtypeStruct(shape, F32)


def hbm(dtype, *shape):
    return pltpu.HBM(shape, dtype)


def split(value):
    high = value.astype(BF16)
    return high, (value - high.astype(F32)).astype(BF16)


def dot3(a, b, dims):
    def one(x, y):
        return lax.dot_general(x, y, dims, preferred_element_type=F32)

    return one(a[0], b[0]) + (one(a[0], b[1]) + one(a[1], b[0]))


def cut_eigenvectors(after_ref, e_ref, out_ref):
    for core in range(2):
        for c in range(NCOL):
            for t in range(4):
                for k in range(8):
                    at = (((k * 2 + core) * NCOL + c) * 4 + t) * 128
                    out_ref[k * NCOL + c, core * 16 + t * 4 : core * 16 + t * 4 + 4, :] = e_ref[:, at : at + 128]


def cut_vectors(w_ref, out_ref, done):
    copies = []
    for core in range(2):
        for c in range(NCOL):
            to = core * NCOL + c
            first = (1 - core) * GROUP
            copies.append(
                pltpu.make_async_copy(
                    w_ref.at[first : first + GROUP, :, c * 512 : c * 512 + 512], out_ref.at[to], done.at[to]
                )
            )
    for copy in copies:
        copy.start()
    for copy in copies:
        copy.wait()


def whole_block(value):
    return jnp.concatenate([value[:NCOL].reshape(NB, 512), value[NCOL:].reshape(NB, 512)], axis=1)


def inner_products(w_ref, e_ref, out_ref, kept_ref, high_ref, low_ref, buf_ref, done):
    keep = pltpu.make_async_copy(w_ref, kept_ref, done.at[0])
    keep.start()
    pieces = pltpu.make_async_copy(e_ref, out_ref.at[:, GROWS:, :], done.at[3])
    pieces.start()
    first = PIECES[0, GROUP - 1, 0][0] // GROWS
    parts = (slice(0, first), slice(first, NCHIP))
    sends = [
        pltpu.make_async_copy(buf_ref.at[part], out_ref.at[part, :GROWS, :], done.at[1 + at])
        for at, part in enumerate(parts)
    ]
    for j in range(GROUP):
        high_ref[j], low_ref[j] = split(whole_block(w_ref[:, j]))
        if j == GROUP - 1:
            sends[0].start()
        for i in range(j + 1):
            value = dot3((high_ref[i], low_ref[i]), (high_ref[j], low_ref[j]), NT)
            for half in range(2):
                at, rows = PIECES[i, j, half]
                at_row = 0
                while at_row < rows:
                    chip, offset = divmod(at + at_row, GROWS)
                    take = min(rows - at_row, GROWS - offset)
                    buf_ref[chip, offset : offset + take, :] = value[at_row : at_row + take, half * 128 : half * 128 + 128]
                    at_row += take
    sends[1].start()
    for copy in (keep, pieces, *sends):
        copy.wait()


def gather_rows(ref, step, first, high_ref, low_ref, value_ref=None, columns=8):
    for t in range(columns):
        for i in range(4):
            value = ref[pl.ds(first + t * 4 + i, NCHIP, stride=step), :]
            high, low = split(value)
            high_ref[i * 64 : i * 64 + 64, t * 128 : t * 128 + 128] = high
            low_ref[i * 64 : i * 64 + 64, t * 128 : t * 128 + 128] = low
            if value_ref is not None:
                value_ref[i * 64 : i * 64 + 64, t * 128 : t * 128 + 128] = value


def scatter_rows(value, block, buf_ref):
    for half in range(2):
        for i in range(4):
            start = (block * 2 + half) * 4 + i
            buf_ref[pl.ds(start, NCHIP, stride=PROWS), :] = value[
                i * 64 : i * 64 + 64, half * 128 : half * 128 + 128
            ]


def local_products(
    core_ref, mine_ref, other_ref, e_ref,
    high_b_ref, low_b_ref, high_a_ref, low_a_ref, x_ref, buf_ref, first_ref, ch_ref, cl_ref,
    eh_ref, el_ref, bh_ref, bl_ref,
):
    core, n = core_ref[0], pl.program_id(0)

    @pl.when(n == 0)
    def _():
        for part in range(2):
            at = pl.ds(part * 512, 512)
            gather_rows(
                e_ref, EROWS, part * 16, eh_ref.at[:, at], el_ref.at[:, at], x_ref.at[:, at], columns=4
            )

    held = (core == 0) == (n < GROUP)
    high, low = split(jnp.where(held, whole_block(mine_ref[:, 0]), whole_block(other_ref[:, 0])))
    value = dot3((eh_ref[...], el_ref[...]), (high, low), NT)

    @pl.when(n < GROUP)
    def _():
        high_b_ref[0], low_b_ref[0] = high, low
        bh_ref[pl.ds(n * NB, NB), :] = high
        bl_ref[pl.ds(n * NB, NB), :] = low
        scatter_rows(value, n, buf_ref)

    @pl.when(n >= GROUP)
    def _():
        high_a_ref[0], low_a_ref[0] = high, low
        first_ref[...] = value
        for j in range(GROUP):
            rows = slice(j * NB, j * NB + NB)
            ch_ref[rows, :], cl_ref[rows, :] = split(
                dot3((bh_ref[rows, :], bl_ref[rows, :]), (high, low), NT)
            )


def sum_chips(buf_ref, rows):
    def add(q, total):
        return total + buf_ref[q, :rows, :]

    return lax.fori_loop(0, NCHIP, add, jnp.zeros((rows, 128), F32), unroll=8)


def spread_rows(part, out_ref):
    def spread(q, carry):
        out_ref[q] = part
        return carry

    lax.fori_loop(0, NCHIP, spread, 0, unroll=8)


def sum_products(buf_ref, out_ref, e_ref, part_ref, done):
    copies = [pltpu.make_async_copy(buf_ref.at[:, GROWS:, :], e_ref, done.at[NCHIP])]
    copies[0].start()
    part_ref[...] = sum_chips(buf_ref, GROWS)
    for q in range(NCHIP):
        copies.append(pltpu.make_async_copy(part_ref, out_ref.at[q], done.at[q]))
        copies[-1].start()
    for copy in copies:
        copy.wait()


def block_of(g_ref, i, j):
    halves = []
    for half in range(2):
        at, rows = PIECES[i, j, half]
        value = g_ref[at : at + rows, :]
        if rows < NB:
            value = jnp.concatenate([value, jnp.zeros((NB - rows, 128), F32)], axis=0)
        halves.append(value)
    return jnp.concatenate(halves, axis=1)


def invert(holder, core_ref, own_ref, sib_ref, *refs):
    high_ref, low_ref, g_ref, held_ref = refs[-4:]
    g_ref[...] = jnp.where(core_ref[0] == holder, own_ref[...], sib_ref[...])
    row = lax.broadcasted_iota(jnp.int32, (NB, NB), 0)
    col = lax.broadcasted_iota(jnp.int32, (NB, NB), 1)
    apart = row ^ col
    for index, (i, j) in enumerate(USES):
        value = block_of(g_ref, i, j)
        if i != j:
            high_ref[index], low_ref[index] = split(value)
            continue
        diagonal = jnp.where(row == col, 0.5 * value, 0.0)
        down = 1.0 / jnp.sum(diagonal, axis=1, keepdims=True)
        across = 1.0 / jnp.sum(diagonal, axis=0, keepdims=True)
        beside = jnp.where((apart == 1) & (row < col), value, 0.0)
        held_ref[i] = jnp.where(row == col, down, 0.0) - down * beside * across
    size = 2
    while size < NB:
        for i in range(GROUP):
            beside = jnp.where((apart >= size) & (apart < 2 * size) & (row < col), block_of(g_ref, i, i), 0.0)
            value = held_ref[i]
            halves = split(value)
            product = dot3(split(dot3(halves, split(beside), NN)), halves, NN)
            held_ref[i] = value - product
        size *= 2
    for i in range(GROUP):
        index = USES.index((i, i))
        high_ref[index], low_ref[index] = split(held_ref[i])


def solve(rows_of, factor, keep):
    found = {}
    for b in range(GROUP - 1, -1, -1):
        rest = jnp.concatenate([rows_of(b * 2), rows_of(b * 2 + 1)], axis=1)
        for later in range(GROUP - 1, b, -1):
            rest = rest - dot3(found[later], factor(b, later), NT)
        value = dot3(split(rest), factor(b, b), NT)
        found[b] = split(value)
        for half in range(2):
            keep(b * 2 + half, value[:, half * 128 : half * 128 + 128])


def solve_own(buf_ref, high_from, low_from, out_ref, high_ref, low_ref, c_ref, done):
    parts = (slice(0, 3), slice(3, len(USES)))
    fetches = []
    for at, part in enumerate(parts):
        fetches.append(pltpu.make_async_copy(high_from.at[part], high_ref.at[part], done.at[0, at]))
        fetches.append(pltpu.make_async_copy(low_from.at[part], low_ref.at[part], done.at[1, at]))
    for fetch in fetches:
        fetch.start()
    c_ref[...] = sum_chips(buf_ref, PROWS)

    def rows_of(t):
        return jnp.concatenate([c_ref[t * 4 : t * 4 + 4, :]] * 2, axis=0)

    def keep(t, value):
        c_ref[t * 4 : t * 4 + 4, :] = value[0:4]

    def factor(i, j):
        index = USES.index((i, j))
        if index in (0, 3):
            for fetch in fetches[0:2] if index == 0 else fetches[2:4]:
                fetch.wait()
        return high_ref[index], low_ref[index]

    solve(rows_of, factor, keep)
    spread_rows(c_ref[...], out_ref)


def correct_projection(c_ref, gh_ref, gl_ref, first_ref, buf_ref, ch_ref, cl_ref):
    gather_rows(c_ref, PROWS, 0, ch_ref, cl_ref)
    for n in range(GROUP):
        at = slice(n * NB, n * NB + NB)
        value = first_ref[:, at] - dot3((ch_ref[...], cl_ref[...]), (gh_ref[:, at], gl_ref[:, at]), NN)
        scatter_rows(value, n, buf_ref)


def updated(n, high_ref, low_ref, x_ref, ch_ref, cl_ref):
    at = slice(n * NB, n * NB + NB)
    vectors = (high_ref[:, :, at].reshape(1024, NB), low_ref[:, :, at].reshape(1024, NB))
    return x_ref[:, at] - dot3((ch_ref[...], cl_ref[...]), vectors, NN)


def update(c_ref, high_ref, low_ref, x_ref, out_ref, ch_ref, cl_ref):
    gather_rows(c_ref, PROWS, 0, ch_ref, cl_ref)
    for n in range(4):
        out_ref[:, n * NB : n * NB + NB] = updated(n, high_ref, low_ref, x_ref, ch_ref, cl_ref)


def update_last(c_ref, high_ref, low_ref, x_ref, out_ref, ch_ref, cl_ref):
    gather_rows(c_ref, PROWS, 0, ch_ref, cl_ref)
    for n in range(4):
        value = updated(n, high_ref, low_ref, x_ref, ch_ref, cl_ref)
        at = n % 2 * NB
        for c in range(NCOL):
            for i in range(4):
                rows = slice(i * 64 + c * 8, i * 64 + c * 8 + 8)
                out_ref[n // 2 * NCOL + c, i * 8 : i * 8 + 8, at : at + NB] = value[rows, :]


def pass_on(after_ref, in_ref, out_ref):
    pass


def place_rows(in_ref, out_ref, held_ref):
    for c in range(NCOL):
        for t in range(4):
            at = c * 512 + t * 128
            for core in range(2):
                for i in range(4):
                    held_ref[pl.ds((c * 4 + t) * 64 + core * 32 + i, 8, stride=4), :] = in_ref[
                        core * NCOL + c, i * 8 : i * 8 + 8, t * 128 : t * 128 + 128
                    ]
            out_ref[:, at : at + 128] = held_ref[(c * 4 + t) * 64 : (c * 4 + t) * 64 + 64, :]


def whole(*shape):
    return pl.BlockSpec(shape, lambda *_: (0,) * len(shape))


def run(kernel, out_shape, out_specs, in_specs, operands, grid=(1,), scratch=(), core=None, flops=0, size=0, limit=32, pin=(), **options):
    operands = [in_hbm(value) if at in pin else value for at, value in enumerate(operands)]
    spec = pltpu.PrefetchScalarGridSpec(
        num_scalar_prefetch=0 if core is None else 1,
        grid=grid,
        in_specs=in_specs,
        out_specs=out_specs,
        scratch_shapes=list(scratch),
    )
    built = pl.pallas_call(
        kernel,
        out_shape=out_shape,
        grid_spec=spec,
        compiler_params=pltpu.CompilerParams(vmem_limit_bytes=limit * 2**20),
        cost_estimate=pl.CostEstimate(flops=flops, bytes_accessed=size, transcendentals=0),
        **options,
    )
    return built(*operands) if core is None else built(core, *operands)


def direct(kernel, out_shape, operands, scratch=(), in_specs=None, out_specs=None, flops=0, size=0, limit=32):
    return pl.pallas_call(
        kernel,
        out_shape=out_shape,
        in_specs=[VMEM] * len(operands) if in_specs is None else in_specs,
        out_specs=jax.tree.map(lambda _: VMEM, out_shape) if out_specs is None else out_specs,
        scratch_shapes=list(scratch),
        compiler_params=pltpu.CompilerParams(vmem_limit_bytes=limit * 2**20),
        cost_estimate=pl.CostEstimate(flops=flops, bytes_accessed=size, transcendentals=0),
    )(*operands)


def in_hbm(value):
    return pltpu.with_memory_space_constraint(value, pltpu.HBM)


def in_vmem(value):
    return pltpu.with_memory_space_constraint(value, pltpu.VMEM)


def exchange(value, axes):
    return lax.all_to_all(value, axes, 0, 0, tiled=True)


def on_device(eigenvectors, reflectors):
    core = lax.axis_index("core").astype(jnp.int32).reshape(1)
    mega = 2**20
    rows_pair = [pltpu.VMEM((256, 1024), BF16)] * 2

    def after(earlier, value, pin=(0,)):
        return run(
            pass_on, jax.ShapeDtypeStruct(value.shape, F32), ANY, [ANY, ANY], (earlier, value), pin=pin, size=1024, input_output_aliases={1: 0}
        )

    vectors = run(
        cut_vectors,
        f32(2 * NCOL, GROUP, 32, 512),
        whole(2 * NCOL, GROUP, 32, 512),
        [HBM],
        (reflectors,),
        pin=(0,),
        scratch=[pltpu.SemaphoreType.DMA((2 * NCOL,))],
        size=8 * mega,
    )
    mine = exchange(vectors, CORE_COLS)
    pieces = run(
        cut_eigenvectors,
        f32(NCHIP, EROWS, 128),
        whole(NCHIP, EROWS, 128),
        [ANY, whole(4, 65536)],
        (mine, eigenvectors),
        size=2 * mega,
    )
    buf, kept = direct(
        inner_products,
        (hbm(F32, NCHIP, STEP, 128), hbm(F32, 2 * NCOL, GROUP, 32, 512)),
        (mine, pieces),
        scratch=[pltpu.VMEM((GROUP, NB, 1024), BF16)] * 2
        + [pltpu.VMEM((NCHIP, GROWS, 128), F32), pltpu.SemaphoreType.DMA((4,))],
        out_specs=(HBM, HBM),
        flops=4 * 10**9,
        size=6 * mega,
    )
    other = lax.ppermute(kept, "core", SWAP)
    arrived = exchange(buf, CHIPS)

    part, spread = run(
        sum_products,
        (hbm(F32, NCHIP, GROWS, 128), hbm(F32, NCHIP, EROWS, 128)),
        (HBM, HBM),
        [whole(NCHIP, STEP, 128)],
        (arrived,),
        scratch=[pltpu.VMEM((GROWS, 128), F32), pltpu.SemaphoreType.DMA((NCHIP + 1,))],
        size=5 * mega,
    )

    block = pl.BlockSpec((2 * NCOL, 1, 32, 512), lambda n, core: (0, lax.rem(n, GROUP), 0, 0))
    early = pl.BlockSpec((1, NB, 1024), lambda n, core: (jnp.minimum(n, GROUP - 1), 0, 0))
    late = pl.BlockSpec((1, NB, 1024), lambda n, core: (jnp.maximum(n - GROUP, 0), 0, 0))
    column = pl.BlockSpec((1024, NB), lambda n, core: (0, jnp.maximum(n - GROUP, 0)))
    split_vectors = hbm(BF16, GROUP, NB, 1024)
    high_b, low_b, high_a, low_a, start, buf, first, cross_high, cross_low = run(
        local_products,
        (
            split_vectors, split_vectors, split_vectors, split_vectors, hbm(F32, 256, 1024),
            hbm(F32, NCHIP * PROWS, 128), hbm(F32, 256, 1024), hbm(BF16, 1024, 1024), hbm(BF16, 1024, 1024),
        ),
        (
            early, early, late, late, whole(256, 1024), whole(NCHIP * PROWS, 128),
            pl.BlockSpec((256, NB), lambda n, core: (0, jnp.maximum(n - GROUP, 0))), column, column,
        ),
        [block, block, whole(NCHIP * EROWS, 128)],
        (kept, other, spread.reshape(NCHIP * EROWS, 128)),
        pin=(0, 1),
        grid=(8,),
        scratch=rows_pair + [pltpu.VMEM((1024, 1024), BF16)] * 2,
        core=core,
        flops=10**10,
        size=24 * mega,
    )
    gram = after(buf, exchange(part, CHIPS)).reshape(ALLROWS, 128)

    count = len(PAIRS)
    gram_sib = lax.ppermute(gram, "core", SWAP)

    def factors_of(holder, later=()):
        return run(
            functools.partial(invert, holder),
            (hbm(BF16, count, NB, NB),) * 2,
            (whole(count, NB, NB),) * 2,
            [whole(ALLROWS, 128)] * 2 + [ANY] * len(later),
            (gram, gram_sib, *later),
            scratch=[pltpu.VMEM((ALLROWS, 128), F32), pltpu.VMEM((GROUP, NB, NB), F32)],
            core=core,
        )

    def coefficients_of(arrived, high, low):
        found = direct(
            solve_own,
            f32(NCHIP, PROWS, 128),
            (arrived, in_hbm(high), in_hbm(low)),
            scratch=[
                pltpu.VMEM((count, NB, NB), BF16),
                pltpu.VMEM((count, NB, NB), BF16),
                pltpu.VMEM((PROWS, 128), F32),
                pltpu.SemaphoreType.DMA((2, 2)),
            ],
            in_specs=[VMEM, HBM, HBM],
            flops=10**8,
            size=5 * mega,
        )
        return exchange(found, CHIPS).reshape(NCHIP * PROWS, 128)

    high, low = factors_of(0, (in_vmem(cross_high), in_vmem(cross_low), in_vmem(first)))
    arrived = after(high, exchange(after(gram, buf, (1,)).reshape(NCHIP, PROWS, 128), CHIPS))
    coefficients = coefficients_of(arrived, high, low)
    buf = direct(
        correct_projection,
        hbm(F32, NCHIP * PROWS, 128),
        (coefficients, cross_high, cross_low, first),
        scratch=rows_pair,
        flops=2 * 10**9,
        size=7 * mega,
    )
    middle = direct(
        update,
        f32(256, 1024),
        (coefficients, high_b, low_b, start),
        scratch=rows_pair,
        flops=2 * 10**9,
        size=7 * mega,
    )
    high, low = factors_of(1)
    arrived = after(middle, after(high, exchange(buf.reshape(NCHIP, PROWS, 128), CHIPS)), ())
    coefficients = coefficients_of(arrived, high, low)
    finished = direct(
        update_last,
        f32(2 * NCOL, 32, 512),
        (coefficients, high_a, low_a, middle),
        scratch=rows_pair,
        flops=2 * 10**9,
        size=7 * mega,
    )
    return run(
        place_rows,
        f32(64, 4096),
        whole(64, 4096),
        [whole(2 * NCOL, 32, 512)],
        (exchange(finished, CORE_COLS),),
        scratch=[pltpu.VMEM((2048, 128), F32)],
        size=2 * mega,
    )


def solution(mesh):
    fine = Mesh(mesh.devices.reshape(SIZES), AXES)
    in_specs = (P(AXES, None), P(None, COLS, ("y", "xl", "core")))
    out_specs = P(COLS, ("y", "xl", "core"))
    return jax.shard_map(on_device, mesh=fine, in_specs=in_specs, out_specs=out_specs, check_vma=False)
```
